32 devices in a mesh: dp: 16 (over z, x, core), outer: 2 (over y).
Axes of the slice: x: 2, y: 2, z: 4, core: 2. Of those that a mesh axis runs over, the one named last changes fastest.
Arguments:
- patches: bfloat16 [128, 256, 768], P(('dp', 'outer')), may hold values from -6 to 6
- lengths: int32 [128], P(('dp', 'outer')), may hold values from 64 to 256, as said below
- leads: int32 [128], P(('dp', 'outer')), may hold values from 0 to 39
- counts: int32 [32], P(('dp', 'outer')), may hold values from 1 to 4, as said below
- cotangent: bfloat16 [128, 256, 768], P(('dp', 'outer')), may hold values from -6 to 6
- norm1_gain: float32 [768], replicated, may hold values from 0.5 to 1.5
- norm1_bias: float32 [768], replicated, may hold values from -1.75 to 1.75
- lead_table: float32 [40, 768], replicated, may hold values from -3 to 3
- w_qkv: bfloat16 [768, 2304], replicated, may hold values from -0.21875 to 0.21875
- bias_query: float32 [768], replicated, may hold values from -1.75 to 1.75
- bias_value: float32 [768], replicated, may hold values from -1.75 to 1.75
- w_out: bfloat16 [768, 768], replicated, may hold values from -0.625 to 0.625
- bias_out: float32 [768], replicated, may hold values from -1.75 to 1.75
- norm2_gain: float32 [768], replicated, may hold values from 0.5 to 1.5
- norm2_bias: float32 [768], replicated, may hold values from -1.75 to 1.75
- w_up: bfloat16 [768, 3072], replicated, may hold values from -0.21875 to 0.21875
- bias_up: float32 [3072], replicated, may hold values from -1.75 to 1.75
- w_down: bfloat16 [3072, 768], replicated, may hold values from -0.109375 to 0.109375
- bias_down: float32 [768], replicated, may hold values from -1.75 to 1.75
Outputs:
- block_out: bfloat16 [128, 256, 768], P(('dp', 'outer'))
- grad_patches: bfloat16 [128, 256, 768], P(('dp', 'outer'))
- grad_norm1_gain: float32 [768], replicated
- grad_norm1_bias: float32 [768], replicated
- grad_lead_table: float32 [40, 768], replicated
- grad_w_qkv: float32 [768, 2304], P('dp')
- grad_bias_query: float32 [768], replicated
- grad_bias_value: float32 [768], replicated
- grad_w_out: float32 [768, 768], P('dp')
- grad_bias_out: float32 [768], replicated
- grad_norm2_gain: float32 [768], replicated
- grad_norm2_bias: float32 [768], replicated
- grad_w_up: float32 [768, 3072], P('dp')
- grad_bias_up: float32 [3072], replicated
- grad_w_down: float32 [3072, 768], P('dp')
- grad_bias_down: float32 [768], replicated
The draws below stay inside these ranges and needn't reach their ends.
Inputs may be any that keep to these rules, and one draw needn't show every extreme that they name: `lengths`: some window is full and some has 64 real patches. `counts`: a device's live windows are its first slots; some device has all 4 live and some one.
All inputs are finite; a program needn't handle non-finite values.
Results may differ from the reference program's by a relative error of at most 0.012.
The reference program's roundings to bfloat16 on the way count: a program that leaves them out, or rounds other values in their place, can miss the bound.
Values sent between devices are 32-bit elements; how exact they have to be, the bound alone decides.
No kernel may reach another device: no remote copies, remote signals or barrier semaphores. Data moves between devices by JAX's collectives and lax.ppermute only.
A program may use at most 192 MiB of HBM per device.

```python
import math
import jax
import jax.numpy as jnp
from jax import lax

D = 768
HEADS = 12
FF = 3072
WIN = 256
NLEAD = 40
SLOTS = 4
WINDOWS = 128
N_DP = 16
N_OUTER = 2


def draw_lengths(key, part):
    key = jax.random.fold_in(key, 11)
    draw_key, full_key, short_key = jax.random.split(key, 3)
    lengths_drawn = jax.random.randint(draw_key, (WINDOWS,), WIN // 4, WIN + 1)
    full_at = jax.random.randint(full_key, (), 0, WINDOWS)
    short_at = (full_at + 1 + jax.random.randint(short_key, (), 0, WINDOWS - 1)) % WINDOWS
    position = jnp.arange(WINDOWS)
    lengths_drawn = jnp.where(position == full_at, WIN, lengths_drawn)
    lengths_drawn = jnp.where(position == short_at, WIN // 4, lengths_drawn)
    return lengths_drawn.astype(jnp.int32)


def draw_counts(key, part):
    key = jax.random.fold_in(key, 23)
    device_total = N_DP * N_OUTER
    draw_key, full_key, short_key = jax.random.split(key, 3)
    counts_drawn = jax.random.randint(draw_key, (device_total,), 1, SLOTS + 1)
    full_at = jax.random.randint(full_key, (), 0, device_total)
    short_at = (full_at + 1 + jax.random.randint(short_key, (), 0, device_total - 1)) % device_total
    position = jnp.arange(device_total)
    counts_drawn = jnp.where(position == full_at, SLOTS, counts_drawn)
    counts_drawn = jnp.where(position == short_at, 1, counts_drawn)
    return counts_drawn.astype(jnp.int32)


def place_ends(result, rng, low, high):
    shape = result.shape
    index_at = [jax.random.randint(jax.random.fold_in(rng, axis), (), 0, shape[axis]) for axis in range(len(shape))]
    result = result.at[tuple(index_at)].set(low)
    longest = shape.index(max(shape))
    index_at[longest] = (index_at[longest] + 1) % shape[longest]
    return result.at[tuple(index_at)].set(high)


def block_levels(own_key, dims, cuts, smallest, largest):
    def one(dim, blocks):
        heights = jax.random.uniform(jax.random.fold_in(jax.random.fold_in(own_key, 6), dim), (blocks,), jnp.float32, smallest / len(cuts), largest / len(cuts))
        return jnp.repeat(jnp.exp(heights), dims[dim] // blocks).reshape((-1,) + (1,) * (len(dims) - dim - 1))

    factor_of = one(*cuts[0])
    for cut in cuts[1:]:
        factor_of = factor_of * one(*cut)
    return factor_of


def bell_draw(key, dims, width, reach, cuts=(), held_as=jnp.bfloat16):
    array = jax.random.normal(key, dims, jnp.float32) * width
    if len(cuts) > 0:
        array = block_levels(key, dims, cuts, -0.22, 0.18) * array
    return jnp.clip(array, min=-reach, max=reach).astype(held_as)


def setup_inputs(seed: int = 0) -> dict:
    key_of = jax.random.split(jax.random.key(seed), 20)
    patches = bell_draw(key_of[0], (WINDOWS, WIN, D), 1.0, 6.0, ((0, 32),))
    lengths = draw_lengths(jax.random.fold_in(key_of[19], 71), 0)
    leads = place_ends(jax.random.randint(key_of[2], (WINDOWS,), 0, NLEAD), jax.random.fold_in(key_of[2], 1), 0, NLEAD - 1).astype(jnp.int32)
    counts = draw_counts(jax.random.fold_in(key_of[19], 71), 0)
    cotangent = bell_draw(key_of[4], (WINDOWS, WIN, D), 1.0, 6.0, ((0, 32),))
    norm1_gain = jnp.clip(1.0 + 0.1 * jax.random.normal(key_of[5], (D,), jnp.float32), 0.5, 1.5)
    norm1_bias = bell_draw(key_of[6], (D,), 0.3, 1.75, (), jnp.float32)
    lead_table = bell_draw(key_of[7], (NLEAD, D), 0.5, 3.0, (), jnp.float32)
    w_qkv = bell_draw(key_of[8], (D, 3 * D), D ** -0.5, 0.21875)
    bias_query = bell_draw(key_of[9], (D,), 0.3, 1.75, (), jnp.float32)
    bias_value = bell_draw(key_of[10], (D,), 0.3, 1.75, (), jnp.float32)
    w_out = bell_draw(key_of[11], (D, D), (D // 8) ** -0.5, 0.625)
    bias_out = bell_draw(key_of[12], (D,), 0.3, 1.75, (), jnp.float32)
    norm2_gain = jnp.clip(1.0 + 0.1 * jax.random.normal(key_of[13], (D,), jnp.float32), 0.5, 1.5)
    norm2_bias = bell_draw(key_of[14], (D,), 0.3, 1.75, (), jnp.float32)
    w_up = bell_draw(key_of[15], (D, FF), D ** -0.5, 0.21875)
    bias_up = bell_draw(key_of[16], (FF,), 0.3, 1.75, (), jnp.float32)
    w_down = bell_draw(key_of[17], (FF, D), FF ** -0.5, 0.109375)
    bias_down = bell_draw(key_of[18], (D,), 0.3, 1.75, (), jnp.float32)
    return {"patches": patches, "lengths": lengths, "leads": leads, "counts": counts, "cotangent": cotangent, "norm1_gain": norm1_gain, "norm1_bias": norm1_bias, "lead_table": lead_table, "w_qkv": w_qkv, "bias_query": bias_query, "bias_value": bias_value, "w_out": w_out, "bias_out": bias_out, "norm2_gain": norm2_gain, "norm2_bias": norm2_bias, "w_up": w_up, "bias_up": bias_up, "w_down": w_down, "bias_down": bias_down}


norm_epsilon = 1e-05
masked_score = -1e+30

@jax.custom_vjp
def low(v):
    return lax.optimization_barrier(v.astype(jnp.bfloat16)).astype(jnp.float32)

@jax.custom_vjp
def low_back(v):
    return v

def low_keep(v):
    return (low(v), None)

def low_pass(kept, grad):
    return (grad,)

def back_keep(v):
    return (v, None)

def back_low(kept, grad):
    return (low(grad),)
low.defvjp(low_keep, low_pass)
low_back.defvjp(back_keep, back_low)

def layer_norm(values_in, norm_gain, norm_bias):
    centre = lax.optimization_barrier(jnp.mean(values_in, axis=-1, keepdims=True))
    centred = values_in - centre
    spread = lax.optimization_barrier(jnp.mean(centred * centred, axis=-1, keepdims=True))
    return centred * lax.rsqrt(spread + norm_epsilon) * norm_gain + norm_bias

def window_block(params, inputs, lead_rows, valid_keys):
    norm1_gain, norm1_bias, lead_table, w_qkv, bias_query, bias_value, w_out, bias_out, norm2_gain, norm2_bias, w_up, bias_up, w_down, bias_down = params
    precise = lax.Precision.HIGHEST
    count, window_len, model_width = inputs.shape
    head_dim = model_width // HEADS
    normed = layer_norm(inputs, norm1_gain, norm1_bias) + lead_rows[:, None, :]
    flat_in = low(normed).reshape(-1, model_width)
    projected = jnp.dot(flat_in, w_qkv, precision=precise, preferred_element_type=jnp.float32)
    shape_heads = (count, window_len, HEADS, head_dim)
    queries = low(low_back(projected[:, :model_width] + bias_query)).reshape(shape_heads)
    keys_low = low(low_back(projected[:, model_width:2 * model_width])).reshape(shape_heads)
    values_low = low(low_back(projected[:, 2 * model_width:] + bias_value)).reshape(shape_heads)
    raw_scores = jnp.einsum('swhd,sthd->shwt', queries, keys_low, precision=precise)
    scores = low_back(raw_scores * 0.125)
    scores = jnp.where(valid_keys[:, None, None, :], scores, masked_score)
    row_max = lax.optimization_barrier(jnp.max(scores, axis=-1, keepdims=True))
    exponent = jnp.exp(scores - row_max)
    probs = exponent / lax.optimization_barrier(jnp.sum(exponent, axis=-1, keepdims=True))
    attended = jnp.einsum('shwt,sthd->swhd', low(probs), values_low, precision=precise)
    attended = low(low_back(attended)).reshape(-1, model_width)
    branch = low_back(jnp.dot(attended, w_out, precision=precise, preferred_element_type=jnp.float32) + bias_out)
    residual = inputs.reshape(-1, model_width) + branch
    normed2 = layer_norm(residual, norm2_gain, norm2_bias)
    pre_up = low_back(jnp.dot(low(normed2), w_up, precision=precise, preferred_element_type=jnp.float32) + bias_up)
    activated = jax.nn.gelu(pre_up, approximate=False)
    pre_down = low_back(jnp.dot(low(activated), w_down, precision=precise, preferred_element_type=jnp.float32) + bias_down)
    return (residual + pre_down).reshape(count, window_len, model_width)

def reference(patches, lengths, leads, counts, cotangent, norm1_gain, norm1_bias, lead_table, w_qkv, bias_query, bias_value, w_out, bias_out, norm2_gain, norm2_bias, w_up, bias_up, w_down, bias_down):
    params = (norm1_gain.astype(jnp.float32), norm1_bias.astype(jnp.float32), lead_table.astype(jnp.float32), w_qkv.astype(jnp.float32), bias_query.astype(jnp.float32), bias_value.astype(jnp.float32), w_out.astype(jnp.float32), bias_out.astype(jnp.float32), norm2_gain.astype(jnp.float32), norm2_bias.astype(jnp.float32), w_up.astype(jnp.float32), bias_up.astype(jnp.float32), w_down.astype(jnp.float32), bias_down.astype(jnp.float32))
    valid_keys = jnp.arange(WIN, dtype=jnp.int32)[None, :] < lengths[:, None]
    slot_index = jnp.arange(WINDOWS, dtype=jnp.int32) % SLOTS
    live_slots = slot_index < jnp.repeat(counts, SLOTS)
    onehot = (leads[:, None] == jnp.arange(NLEAD, dtype=jnp.int32)[None, :]).astype(jnp.float32)
    lead_totals = lax.optimization_barrier(jnp.sum(onehot * live_slots[:, None].astype(jnp.float32), axis=0))
    window_total = lax.optimization_barrier(jnp.sum(onehot * lead_totals[None, :], axis=1))
    window_scale = jnp.where(live_slots, 1.0 / jnp.maximum(window_total, 1.0), 0.0)
    inputs = patches.astype(jnp.float32)
    group_size = math.gcd(WINDOWS, 16)
    group_count = WINDOWS // group_size

    def forward(inputs_all, params_all):
        lead_rows = params_all[2][leads]
        grouped = (inputs_all.reshape(group_count, group_size, WIN, -1), lead_rows.reshape(group_count, group_size, -1), valid_keys.reshape(group_count, group_size, WIN))

        def one_group(pieces):
            return jax.checkpoint(window_block)(params_all, pieces[0], pieces[1], pieces[2])
        return lax.map(one_group, grouped).reshape(inputs_all.shape)
    block_out, pullback = jax.vjp(forward, inputs, params)
    weighting = (window_scale[:, None] * valid_keys.astype(jnp.float32))[:, :, None]
    grad_inputs, grad_params = pullback(cotangent.astype(jnp.float32) * weighting)
    return (block_out.astype(jnp.bfloat16), grad_inputs.astype(jnp.bfloat16), grad_params[0], grad_params[1], grad_params[2], grad_params[3], grad_params[4], grad_params[5], grad_params[6], grad_params[7], grad_params[8], grad_params[9], grad_params[10], grad_params[11], grad_params[12], grad_params[13])
```

```python
import jax
import jax.numpy as jnp
from jax import lax
from jax.sharding import PartitionSpec as P

HEADS = 12


norm_epsilon = 1e-05
masked_score = -1e30


def layer_norm(values_in, norm_gain, norm_bias):
    centre = jnp.mean(values_in, axis=-1, keepdims=True)
    centred = values_in - centre
    spread = jnp.mean(centred * centred, axis=-1, keepdims=True)
    return centred * lax.rsqrt(spread + norm_epsilon) * norm_gain + norm_bias


def exact_gelu(pre_values):
    return jax.nn.gelu(pre_values, approximate=False)


def swap(values, axis, bit):
    size = lax.axis_size(axis)
    return lax.ppermute(values, axis, [(i, i ^ (1 << bit)) for i in range(size)])


def bit_of(axis, bit):
    return lax.rem(lax.div(lax.axis_index(axis), 1 << bit), 2)


def dp_bits():
    return lax.axis_size("dp").bit_length() - 1


def sum_small(values):
    for bit in range(dp_bits()):
        values = values + swap(values, "dp", bit)
    return values + swap(values, "outer", 0)


def part_orders(bit_count):
    rest = list(range(3, bit_count))
    return (
        [("dp", 1), ("outer", 0), ("dp", 2)] + [("dp", b) for b in rest],
        [("outer", 0), ("dp", 2), ("dp", 1)] + [("dp", b) for b in rest],
        [("dp", 2), ("dp", 1), ("outer", 0)] + [("dp", b) for b in rest],
    )


def halve(values, dims, step):
    axis, bit = step
    place = dims.index(step)
    mine = bit_of(axis, bit)
    keep = lax.dynamic_index_in_dim(values, mine, place, keepdims=False)
    send = lax.dynamic_index_in_dim(values, 1 - mine, place, keepdims=False)
    left = dims[:place] + dims[place + 1 :]
    return keep + swap(send, axis, bit), left


def scatter_sum(matrix):
    bit_count = dp_bits()
    rows, columns = matrix.shape
    share = rows // lax.axis_size("dp")
    dims = [("dp", b) for b in range(bit_count - 1, -1, -1)] + [("outer", 0)]
    values = matrix.reshape((2,) * bit_count + (2, share // 2, columns))
    values, dims = halve(values, dims, ("dp", 0))
    third = columns // 3
    pieces = []
    for index, order in enumerate(part_orders(bit_count)):
        part = lax.slice_in_dim(values, index * third, (index + 1) * third, axis=values.ndim - 1)
        left = dims
        for step in order:
            part, left = halve(part, left, step)
        pieces.append(part)
    mine = jnp.concatenate(pieces, axis=1)
    other = swap(mine, "outer", 0)
    first = lax.axis_index("outer") == 0
    return jnp.concatenate([jnp.where(first, mine, other), jnp.where(first, other, mine)], axis=0)


def per_device(
    patches,
    lengths,
    leads,
    counts,
    cotangent,
    norm1_gain,
    norm1_bias,
    lead_table,
    w_qkv,
    bias_query,
    bias_value,
    w_out,
    bias_out,
    norm2_gain,
    norm2_bias,
    w_up,
    bias_up,
    w_down,
    bias_down,
):
    slot_count, window_len, model_width = patches.shape
    row_count = slot_count * window_len
    head_dim = model_width // HEADS
    lead_count = lead_table.shape[0]
    precise = lax.Precision.HIGHEST
    valid_keys = jnp.arange(window_len, dtype=jnp.int32)[None, :] < lengths[:, None]
    live_slots = jnp.arange(slot_count, dtype=jnp.int32) < counts[0]
    onehot = (leads[:, None] == jnp.arange(lead_count, dtype=jnp.int32)[None, :]).astype(
        jnp.float32
    )
    local_hist = jnp.sum(onehot * live_slots[:, None].astype(jnp.float32), axis=0)
    lead_totals = sum_small(local_hist)
    window_total = jnp.sum(onehot * lead_totals[None, :], axis=1)
    window_scale = jnp.where(live_slots, 1.0 / jnp.maximum(window_total, 1.0), 0.0)
    lead_rows = jnp.dot(onehot, lead_table, precision=precise, preferred_element_type=jnp.float32)
    inputs = patches.astype(jnp.float32)

    def first_norm(inputs_in, norm_gain, norm_bias, lead_part):
        return layer_norm(inputs_in, norm_gain, norm_bias) + lead_part[:, None, :]

    normed, first_back = jax.vjp(first_norm, inputs, norm1_gain, norm1_bias, lead_rows)
    normed_low = normed.astype(jnp.bfloat16).reshape(row_count, model_width)
    projected = jnp.dot(normed_low, w_qkv, preferred_element_type=jnp.float32)
    shape_heads = (slot_count, window_len, HEADS, head_dim)
    queries = (projected[:, :model_width] + bias_query).astype(jnp.bfloat16).reshape(shape_heads)
    keys_low = projected[:, model_width : 2 * model_width].astype(jnp.bfloat16).reshape(shape_heads)
    values_low = (
        (projected[:, 2 * model_width :] + bias_value).astype(jnp.bfloat16).reshape(shape_heads)
    )
    key_mask = valid_keys[:, None, None, :]

    def compute_scores():
        raw_scores = jnp.einsum(
            "swhd,sthd->shwt", queries, keys_low, preferred_element_type=jnp.float32
        )
        return jnp.where(key_mask, raw_scores * 0.125, masked_score)

    scores = compute_scores()
    row_max = jnp.max(scores, axis=-1, keepdims=True)
    exponent = jnp.exp(scores - row_max)
    row_total = jnp.sum(exponent, axis=-1, keepdims=True)
    probs_low = (exponent / row_total).astype(jnp.bfloat16)
    log_total = row_max + jnp.log(row_total)
    attended = jnp.einsum(
        "shwt,sthd->swhd", probs_low, values_low, preferred_element_type=jnp.float32
    )
    attended_low = attended.astype(jnp.bfloat16).reshape(row_count, model_width)
    branch = jnp.dot(attended_low, w_out, preferred_element_type=jnp.float32) + bias_out
    residual = inputs.reshape(row_count, model_width) + branch

    def second_norm(residual_in, norm_gain, norm_bias):
        return layer_norm(residual_in, norm_gain, norm_bias)

    normed2, second_back = jax.vjp(second_norm, residual, norm2_gain, norm2_bias)
    normed2_low = normed2.astype(jnp.bfloat16)
    pre_up = jnp.dot(normed2_low, w_up, preferred_element_type=jnp.float32) + bias_up
    activated, gelu_back = jax.vjp(exact_gelu, pre_up)
    activated_low = activated.astype(jnp.bfloat16)
    final = (
        residual + jnp.dot(activated_low, w_down, preferred_element_type=jnp.float32) + bias_down
    )
    block_out = final.astype(jnp.bfloat16).reshape(slot_count, window_len, model_width)
    weighting = (window_scale[:, None] * valid_keys.astype(jnp.float32))[:, :, None]
    grad_out = (cotangent.astype(jnp.float32) * weighting).reshape(row_count, model_width)
    grad_down = grad_out.astype(jnp.bfloat16)
    grad_w_down = jnp.einsum(
        "rf,rd->fd", activated_low, grad_down, preferred_element_type=jnp.float32
    )
    grad_bias_down = jnp.sum(grad_down.astype(jnp.float32), axis=0)
    grad_act = jnp.einsum("rd,fd->rf", grad_down, w_down, preferred_element_type=jnp.float32)
    grad_pre_up = gelu_back(grad_act)[0]
    grad_up = grad_pre_up.astype(jnp.bfloat16)
    grad_w_up = jnp.einsum("rd,rf->df", normed2_low, grad_up, preferred_element_type=jnp.float32)
    grad_bias_up = jnp.sum(grad_up.astype(jnp.float32), axis=0)
    grad_normed2 = jnp.einsum("rf,df->rd", grad_up, w_up, preferred_element_type=jnp.float32)
    grad_resid_norm, grad_norm2_gain, grad_norm2_bias = second_back(grad_normed2)
    grad_residual = grad_out + grad_resid_norm
    grad_branch = grad_residual.astype(jnp.bfloat16)
    grad_w_out = jnp.einsum(
        "re,rd->ed", attended_low, grad_branch, preferred_element_type=jnp.float32
    )
    grad_bias_out = jnp.sum(grad_branch.astype(jnp.float32), axis=0)
    grad_attended = jnp.einsum("rd,ed->re", grad_branch, w_out, preferred_element_type=jnp.float32)
    grad_attended = grad_attended.astype(jnp.bfloat16).reshape(shape_heads)
    probs_again = jnp.exp(compute_scores() - log_total)
    probs_again_low = probs_again.astype(jnp.bfloat16)
    grad_probs = jnp.einsum(
        "swhd,sthd->shwt", grad_attended, values_low, preferred_element_type=jnp.float32
    )
    grad_values = jnp.einsum(
        "shwt,swhd->sthd", probs_again_low, grad_attended, preferred_element_type=jnp.float32
    )
    grad_scores = probs_again * (
        grad_probs - jnp.sum(grad_probs * probs_again, axis=-1, keepdims=True)
    )
    grad_scores_low = grad_scores.astype(jnp.bfloat16)
    grad_queries = (
        jnp.einsum("shwt,sthd->swhd", grad_scores_low, keys_low, preferred_element_type=jnp.float32)
        * 0.125
    )
    grad_keys = (
        jnp.einsum("shwt,swhd->sthd", grad_scores_low, queries, preferred_element_type=jnp.float32)
        * 0.125
    )
    grad_projected = jnp.concatenate(
        [
            grad_queries.reshape(row_count, model_width).astype(jnp.bfloat16),
            grad_keys.reshape(row_count, model_width).astype(jnp.bfloat16),
            grad_values.reshape(row_count, model_width).astype(jnp.bfloat16),
        ],
        axis=1,
    )
    grad_w_qkv = jnp.einsum(
        "rd,re->de", normed_low, grad_projected, preferred_element_type=jnp.float32
    )
    grad_bias_query = jnp.sum(grad_projected[:, :model_width].astype(jnp.float32), axis=0)
    grad_bias_value = jnp.sum(grad_projected[:, 2 * model_width :].astype(jnp.float32), axis=0)
    grad_normed = jnp.einsum("re,de->rd", grad_projected, w_qkv, preferred_element_type=jnp.float32)
    grad_normed = grad_normed.reshape(slot_count, window_len, model_width)
    grad_inputs_norm, grad_norm1_gain, grad_norm1_bias, grad_lead_rows = first_back(grad_normed)
    grad_lead_table = jnp.einsum("sl,sd->ld", onehot, grad_lead_rows, precision=precise)
    grad_patches = (
        grad_residual.reshape(slot_count, window_len, model_width) + grad_inputs_norm
    ).astype(jnp.bfloat16)
    vectors = (
        grad_norm1_gain,
        grad_norm1_bias,
        grad_bias_query,
        grad_bias_value,
        grad_bias_out,
        grad_norm2_gain,
        grad_norm2_bias,
        grad_bias_down,
    )
    stacked = jnp.concatenate(
        [jnp.stack(vectors), grad_bias_up.reshape(-1, model_width), grad_lead_table], axis=0
    )
    small = sum_small(stacked)
    up_rows = grad_bias_up.shape[0] // model_width
    sum_down = scatter_sum(grad_w_down)
    sum_up = scatter_sum(grad_w_up)
    sum_last = scatter_sum(jnp.concatenate([grad_w_out, grad_w_qkv], axis=1))
    return (
        block_out,
        grad_patches,
        small[0],
        small[1],
        small[8 + up_rows :],
        sum_last[:, model_width:],
        small[2],
        small[3],
        sum_last[:, :model_width],
        small[4],
        small[5],
        small[6],
        sum_up,
        small[8 : 8 + up_rows].reshape(-1),
        sum_down,
        small[7],
    )


def solution(mesh):
    placed = (
        P(("dp", "outer"), None, None),
        P(("dp", "outer")),
        P(("dp", "outer")),
        P(("dp", "outer")),
        P(("dp", "outer"), None, None),
        P(),
        P(),
        P(),
        P(),
        P(),
        P(),
        P(),
        P(),
        P(),
        P(),
        P(),
        P(),
        P(),
        P(),
    )
    return jax.shard_map(
        per_device,
        mesh=mesh,
        in_specs=placed,
        out_specs=(
            P(("dp", "outer"), None, None),
            P(("dp", "outer"), None, None),
            P(),
            P(),
            P(),
            P("dp", None),
            P(),
            P(),
            P("dp", None),
            P(),
            P(),
            P(),
            P("dp", None),
            P(),
            P("dp", None),
            P(),
        ),
        check_vma=False,
    )
```

```python
import jax
import jax.numpy as jnp
from jax import lax
from jax.experimental import pallas as pl
from jax.experimental.pallas import tpu as pltpu
from jax.sharding import PartitionSpec as P

HEADS = 12
FORWARD_GROUP, BACK_GROUP = 2, 4
LAST_SHARES = (1280, 1280, 512)
NB = 100
VMEM_BYTES = 62 * 1024 * 1024


norm_epsilon = 1e-05
masked_score = -1e30

density_scale = 0.3989422804014327


def dot_nn(a, b):
    return lax.dot_general(a, b, (((1,), (0,)), ((), ())), preferred_element_type=jnp.float32)


def dot_nt(a, b):
    return lax.dot_general(a, b, (((1,), (1,)), ((), ())), preferred_element_type=jnp.float32)


def dot_tn(a, b):
    return lax.dot_general(a, b, (((0,), (0,)), ((), ())), preferred_element_type=jnp.float32)


def normalise(values):
    centre = jnp.mean(values, axis=-1, keepdims=True)
    centred = values - centre
    spread = jnp.mean(centred * centred, axis=-1, keepdims=True)
    inverse = lax.rsqrt(spread + norm_epsilon)
    return centred * inverse, inverse


def normalise_back(grad, unit, inverse):
    first = jnp.mean(grad, axis=-1, keepdims=True)
    second = jnp.mean(grad * unit, axis=-1, keepdims=True)
    return inverse * (grad - first - unit * second)


def column_sum(values):
    return jnp.sum(values, axis=0, keepdims=True)


def gelu_pair(pre):
    normal = 0.5 + 0.5 * lax.erf(pre * 0.7071067811865476)
    return pre * normal, normal + pre * (density_scale * jnp.exp(-0.5 * (pre * pre)))


def line(vector):
    return vector[...].reshape(1, -1)


def project_kernel(
    leads, patches, gain, bias, bias_query, bias_value, lead_table, w_qkv, normed, qkv
):
    window = pl.program_id(0)
    width = patches.shape[-1]
    unit, _ = normalise(patches[0].astype(jnp.float32))
    lead_row = lead_table[pl.ds(leads[window], 1), :]
    low = (unit * line(gain) + line(bias) + lead_row).astype(jnp.bfloat16)
    normed[...] = low
    queries = dot_nn(low, w_qkv[:, :width]) + line(bias_query)
    qkv[:, :width] = queries.astype(jnp.bfloat16) * 0.125
    qkv[:, width : 2 * width] = dot_nn(low, w_qkv[:, width : 2 * width]).astype(jnp.bfloat16)
    values = dot_nn(low, w_qkv[:, 2 * width :]) + line(bias_value)
    qkv[:, 2 * width :] = values.astype(jnp.bfloat16)


def each_alone(columns, place):
    zero = jnp.zeros_like(columns)
    return jnp.concatenate([jnp.where(place == i, columns, zero) for i in range(columns.shape[1] // 64)], axis=0)


def own_columns(stacked, place):
    rows = place.shape[0]
    joined = stacked[:rows]
    for i in range(1, stacked.shape[1] // 64):
        joined = jnp.where(place == i, stacked[i * rows : (i + 1) * rows], joined)
    return joined


def attend_kernel(
    lengths,
    patches,
    qkv,
    w_out,
    bias_out,
    gain,
    bias,
    attended,
    residual,
    normed2,
    turned,
    log_total,
):
    window = pl.program_id(0)
    _, rows, width = patches.shape
    keys_at = lax.broadcasted_iota(jnp.int32, (rows, 1), 0)
    blocked = jnp.where(keys_at < lengths[window], 0.0, masked_score)
    span = FORWARD_GROUP * 64
    place = lax.broadcasted_iota(jnp.int32, (rows, span), 1) // 64
    for at in range(0, width, span):
        query = each_alone(qkv[:, at : at + span], place)
        key = qkv[:, width + at : width + at + span]
        value = qkv[:, 2 * width + at : 2 * width + at + span]
        scores = dot_nt(key, query) + blocked
        top = jnp.max(scores, axis=0, keepdims=True)
        exponent = jnp.exp(scores - top)
        total = jnp.sum(exponent, axis=0, keepdims=True)
        probs = (exponent * (1.0 / total)).astype(jnp.bfloat16)
        out = own_columns(dot_tn(probs, value), place)
        attended[:, at : at + span] = out.astype(jnp.bfloat16)
        log_sum = top + jnp.log(total)
        for i in range(FORWARD_GROUP):
            head = at // 64 + i
            log_total[0, head : head + 1, :] = log_sum[:, i * rows : (i + 1) * rows]
    branch = dot_nn(attended[...], w_out[...]) + line(bias_out)
    held = patches[0].astype(jnp.float32) + branch
    residual[...] = held
    unit, _ = normalise(held)
    low = (unit * line(gain) + line(bias)).astype(jnp.bfloat16)
    normed2[...] = low
    turned[...] = low.T


def store_halves(result, here, keep, send):
    if keep.ndim == 2:
        keep[...] = result
        send[...] = jnp.zeros_like(send)
        return
    blocks, share, columns = keep.shape
    split = result.reshape(blocks, 2, share, columns)
    first, second = split[:, 0], split[:, 1]
    keep[...] = jnp.where(here == 0, first, second)
    send[...] = jnp.where(here == 0, second, first)


def mlp_kernel(
    lengths,
    scales,
    here,
    cotangent,
    normed2,
    w_up,
    bias_up,
    activated,
    slope,
    grad_down,
    keep,
    send,
):
    windows, rows, width = cotangent.shape
    step = pl.program_id(0)

    @pl.when(step == 0)
    def _():
        row = lax.broadcasted_iota(jnp.int32, (rows, 1), 0)
        for window in range(windows):
            weight = jnp.where(row < lengths[window], scales[window], 0.0)
            grad = (cotangent[window].astype(jnp.float32) * weight).astype(jnp.bfloat16)
            grad_down[window * rows : (window + 1) * rows, :] = grad

    for window in range(windows):
        at = slice(window * rows, (window + 1) * rows)
        pre = dot_nn(normed2[at, :], w_up[...]) + bias_up[pl.ds(step, 1), :]
        out, steep = gelu_pair(pre)
        out = out.astype(jnp.bfloat16)
        activated[at, :] = out
        slope[at, :] = steep.astype(jnp.bfloat16)
    store_halves(dot_tn(activated[...], grad_down[...]), here[0], keep, send)


def mlp_back_kernel(
    here, grad_down, slope, turned, w_up, w_down, grad_bias_up, grad_normed2, keep, send
):
    step = pl.program_id(0)

    @pl.when(step == 0)
    def _():
        grad_normed2[...] = jnp.zeros_like(grad_normed2)

    grad_act = dot_nt(grad_down[...], w_down[...])
    grad_up = (grad_act * slope[...].astype(jnp.float32)).astype(jnp.bfloat16)
    grad_bias_up[0] = column_sum(grad_up.astype(jnp.float32))
    store_halves(dot_nn(turned[...], grad_up), here[0], keep, send)
    grad_normed2[...] += dot_nt(grad_up, w_up[...])


def middle_back_kernel(
    lengths,
    scales,
    here,
    cotangent,
    residual,
    grad_normed2,
    attended,
    w_out,
    gain,
    head_rows,
    grad_residual,
    grad_attended,
    delta,
    sums,
    branch_low,
):
    window = pl.program_id(0)
    _, rows, width = cotangent.shape

    @pl.when(window == 0)
    def _():
        sums[...] = jnp.zeros_like(sums)

    row = lax.broadcasted_iota(jnp.int32, (rows, 1), 0)
    weight = jnp.where(row < lengths[window], scales[window], 0.0)
    grad_out = cotangent[0].astype(jnp.float32) * weight
    unit, inverse = normalise(residual[...])
    grad_norm = grad_normed2[...]
    held = grad_out + normalise_back(grad_norm * line(gain), unit, inverse)
    grad_residual[...] = held
    branch = held.astype(jnp.bfloat16)
    branch_low[...] = branch
    sums[0:1, :] += column_sum(grad_norm * unit)
    sums[1:2, :] += column_sum(grad_norm)
    sums[2:3, :] += column_sum(branch.astype(jnp.float32))
    sums[3:4, :] += column_sum(grad_out.astype(jnp.bfloat16).astype(jnp.float32))
    grad_att = dot_nt(branch, w_out[...]).astype(jnp.bfloat16)
    grad_attended[...] = grad_att
    product = grad_att.astype(jnp.float32) * attended[...].astype(jnp.float32)
    high = product.astype(jnp.bfloat16)
    low = (product - high.astype(jnp.float32)).astype(jnp.bfloat16)
    delta[0] = dot_nt(head_rows[...], high) + dot_nt(head_rows[...], low)


def attend_back_kernel(
    lengths,
    here,
    queries,
    keys,
    values,
    grad_attended,
    normed,
    log_total,
    delta,
    attended,
    branch,
    grad_projected,
    sums,
    keep,
    send,
    grad_w,
):
    window = pl.program_id(0)
    rows, width = queries.shape

    @pl.when(window == 0)
    def _():
        grad_w[...] = jnp.zeros_like(grad_w)
        sums[...] = jnp.zeros_like(sums)

    row = lax.broadcasted_iota(jnp.int32, (rows, 1), 0)
    blocked = jnp.where(row < lengths[window], 0.0, masked_score)
    span = BACK_GROUP * 64
    place = lax.broadcasted_iota(jnp.int32, (rows, span), 1) // 64
    for at in range(0, width, span):
        query = each_alone(queries[:, at : at + span], place)
        key = keys[:, at : at + span]
        value = values[:, at : at + span]
        grad_group = each_alone(grad_attended[:, at : at + span], place)
        heads = range(at // 64, at // 64 + BACK_GROUP)
        totals = jnp.concatenate([log_total[0, h : h + 1, :] for h in heads], axis=1)
        shift = jnp.concatenate([delta[0, h : h + 1, :] for h in heads], axis=1)
        scores = dot_nt(key, query) + blocked
        probs = jnp.exp(scores - totals)
        grad_probs = dot_nt(value, grad_group)
        grad_scores = (probs * (grad_probs - shift)).astype(jnp.bfloat16)
        grad_query = own_columns(dot_tn(grad_scores, key), place) * 0.125
        grad_key = dot_nn(grad_scores, query)
        grad_value = dot_nn(probs.astype(jnp.bfloat16), grad_group)
        for index, grad in enumerate((grad_query, grad_key, grad_value)):
            to = index * width + at
            grad_projected[:, to : to + span] = grad.astype(jnp.bfloat16)
    grad_w[:, : 3 * width] += dot_tn(normed[...], grad_projected[...])
    grad_w[:, 3 * width :] += dot_tn(attended[...], branch[...])
    sums[0:1, :] += column_sum(grad_projected[:, :width].astype(jnp.float32))
    sums[1:2, :] += column_sum(grad_projected[:, 2 * width :].astype(jnp.float32))

    @pl.when(window == pl.num_programs(0) - 1)
    def _():
        store_halves(grad_w[...], here[0], keep, send)


def norm_back_kernel(
    leads, patches, grad_residual, grad_projected, w_qkv, gain, grad_patches, sums, grad_leads
):
    window = pl.program_id(0)

    @pl.when(window == 0)
    def _():
        sums[...] = jnp.zeros_like(sums)
        grad_leads[...] = jnp.zeros_like(grad_leads)

    grad_norm = dot_nt(grad_projected[...], w_qkv[...])
    unit, inverse = normalise(patches[0].astype(jnp.float32))
    back = normalise_back(grad_norm * line(gain), unit, inverse)
    grad_patches[0] = (grad_residual[...] + back).astype(jnp.bfloat16)
    total = column_sum(grad_norm)
    sums[0:1, :] += column_sum(grad_norm * unit)
    sums[1:2, :] += total
    grad_leads[pl.ds(leads[window], 1), :] += total


def block_out_kernel(activated, w_down, bias_down, residual, block_out):
    final = residual[...] + dot_nn(activated[...], w_down[...]) + line(bias_down)
    block_out[0] = final.astype(jnp.bfloat16)


Z1, Z0, X, Y = range(4)
LINKS = (("dp", 3), ("dp", 2), ("dp", 1), ("outer", 0))


def split_kernel(pairs, parts, axes, merge, gridded, bits, *refs):
    outs = refs[2 * len(pairs) :]
    start = 0
    for index, (pieces, axis) in enumerate(zip(parts, axes)):
        send, keep = outs[:2] if merge else outs[2 * index : 2 * index + 2]
        if not merge:
            start = 0
        mine = bits[axis]
        for pair, first, width in pieces:
            held, come = refs[2 * pair], refs[2 * pair + 1]
            at = [slice(None)] * len(held.shape)
            if gridded:
                at[0] = 0
            at[-1] = slice(first, first + width)
            place = pairs[pair].index(axis)
            for out, side in ((send, 1 - mine), (keep, mine)):
                at[place] = side
                value = held[tuple(at)] + come[tuple(at)]
                to = (Ellipsis, slice(start, start + width))
                out[(0,) + to if gridded else to] = value
            start += width


def place_kernel(moves, bits, own, other, *outs):
    rows = own.shape[0]
    mine = bits[Y]
    for out, to, start, width in moves:
        for value, side in ((own, mine), (other, 1 - mine)):
            outs[out][pl.ds(side * rows, rows), to : to + width] = value[:, start : start + width]


def swap(values, axis, bit):
    size = lax.axis_size(axis)
    return lax.ppermute(values, axis, [(i, i ^ (1 << bit)) for i in range(size)])


def bit_of(axis, bit):
    return lax.rem(lax.div(lax.axis_index(axis), 1 << bit), 2)


def dp_bits():
    return lax.axis_size("dp").bit_length() - 1


def sum_small(values):
    for bit in reversed(range(dp_bits())):
        values = values + swap(values, "dp", bit)
    return values + swap(values, "outer", 0)


def exchange(values, dp_mask, outer_mask):
    inner = lax.axis_size("outer")
    size = lax.axis_size("dp") * inner
    flip = dp_mask * inner + outer_mask
    return lax.ppermute(values, ("dp", "outer"), [(i, i ^ flip) for i in range(size)])


def count_rounds(values):
    steps = [(1 << bit, 0) for bit in range(1, dp_bits())] + [(0, 1)]
    rounds = [[(1, 0)]] + [steps[at : at + 2] for at in range(0, len(steps), 2)]
    for group in rounds:
        flips = list(group)
        if len(group) == 2:
            flips.append((group[0][0] | group[1][0], group[0][1] | group[1][1]))
        values = values + sum(exchange(values, *flip) for flip in flips)
        yield values


def part_orders(bit_count):
    rest = list(range(3, bit_count))
    return (
        [("dp", 1), ("outer", 0), ("dp", 2)] + [("dp", b) for b in rest],
        [("outer", 0), ("dp", 2), ("dp", 1)] + [("dp", b) for b in rest],
        [("dp", 2), ("dp", 1), ("outer", 0)] + [("dp", b) for b in rest],
    )


def halve(values, dims, step):
    axis, bit = step
    place = dims.index(step)
    mine = bit_of(axis, bit)
    keep = lax.dynamic_index_in_dim(values, mine, place, keepdims=False)
    send = lax.dynamic_index_in_dim(values, 1 - mine, place, keepdims=False)
    left = dims[:place] + dims[place + 1 :]
    return keep + swap(send, axis, bit), left


def scatter_sum(matrix):
    bit_count = dp_bits()
    rows, columns = matrix.shape
    share = rows // lax.axis_size("dp")
    dims = [("dp", b) for b in range(bit_count - 1, -1, -1)] + [("outer", 0)]
    values = matrix.reshape((2,) * bit_count + (2, share // 2, columns))
    values, dims = halve(values, dims, ("dp", 0))
    third = columns // 3
    pieces = []
    for index, order in enumerate(part_orders(bit_count)):
        part = lax.slice_in_dim(values, index * third, (index + 1) * third, axis=values.ndim - 1)
        left = dims
        for step in order:
            part, left = halve(part, left, step)
        pieces.append(part)
    mine = jnp.concatenate(pieces, axis=1)
    other = swap(mine, "outer", 0)
    first = lax.axis_index("outer") == 0
    return jnp.concatenate([jnp.where(first, mine, other), jnp.where(first, other, mine)], axis=0)


def per_device(
    patches,
    lengths,
    leads,
    counts,
    cotangent,
    norm1_gain,
    norm1_bias,
    lead_table,
    w_qkv,
    bias_query,
    bias_value,
    w_out,
    bias_out,
    norm2_gain,
    norm2_bias,
    w_up,
    bias_up,
    w_down,
    bias_down,
):
    slots, rows, width = patches.shape
    total = slots * rows
    hidden = w_up.shape[1]
    lead_count = lead_table.shape[0]
    steps = hidden // width
    f32, bf16 = jnp.float32, jnp.bfloat16
    parts = lax.axis_size("dp")
    share = width // parts
    fast = parts == 16 and share % 16 == 0

    smem = pl.BlockSpec(memory_space=pltpu.SMEM)
    params = pltpu.CompilerParams(vmem_limit_bytes=VMEM_BYTES)

    def whole(*shape):
        return pl.BlockSpec(shape, lambda *i: (0,) * len(shape))

    def by_window(columns, at=0):
        return pl.BlockSpec((rows, columns), lambda i: (i, at))

    def call(kernel, grid, inputs, outs, scratch=(), after=(), carry=(), micros=0):
        count, extra, carried = len(inputs), len(after) + len(carry), len(carry)
        made = count + extra + len(outs)

        def body(*refs):
            kernel(*refs[:count], *refs[count + extra : made], *refs[made + carried :])

        anywhere = pl.BlockSpec(memory_space=pl.ANY)
        return pl.pallas_call(
            body,
            grid=grid,
            in_specs=[spec for spec, _ in inputs] + [anywhere] * extra,
            out_specs=[spec for spec, _, _ in outs] + [anywhere] * carried,
            out_shape=[jax.ShapeDtypeStruct(shape, dtype) for _, shape, dtype in outs]
            + [jax.ShapeDtypeStruct(value.shape, value.dtype) for value in carry],
            input_output_aliases={
                count + len(after) + i: len(outs) + i for i in range(carried)
            },
            scratch_shapes=scratch,
            compiler_params=params,
            cost_estimate=pl.CostEstimate(
                flops=int(micros * 1.15e9), bytes_accessed=0, transcendentals=0
            ),
        )(*[value for _, value in inputs], *after, *carry)

    live = jnp.arange(slots, dtype=jnp.int32) < counts[0]
    onehot = (leads[:, None] == jnp.arange(lead_count, dtype=jnp.int32)[None, :]).astype(f32)
    rounds = count_rounds(jnp.sum(onehot * live[:, None].astype(f32), axis=0))
    counted = next(rounds)

    dp_at, outer_at = lax.axis_index("dp"), lax.axis_index("outer")
    here = lax.rem(dp_at, 2).reshape(1)
    bits = jnp.stack([bit_of("dp", 3), bit_of("dp", 2), bit_of("dp", 1), outer_at])
    def flat(vector):
        return whole(*vector.shape), vector

    by_slot = pl.BlockSpec((1, rows, width), lambda i: (i, 0, 0))
    by_head = pl.BlockSpec((1, 16, rows), lambda i: (i, 0, 0))

    def halves(blocks, columns, grid_axis=None):
        if not fast:
            spec = pl.BlockSpec((width, columns), lambda i: (0, 0))
            return [(spec, (width, columns), f32), (whole(8, 128), (8, 128), f32)]
        shape = (parts // 2, share, columns)
        return [(whole(*shape), shape, f32)] * 2

    normed, qkv = call(
        project_kernel,
        (slots,),
        [
            (smem, leads),
            (by_slot, patches),
            flat(norm1_gain),
            flat(norm1_bias),
            flat(bias_query),
            flat(bias_value),
            (whole(*lead_table.shape), lead_table),
            (whole(*w_qkv.shape), w_qkv),
        ],
        [
            (by_window(width), (total, width), bf16),
            (by_window(3 * width), (total, 3 * width), bf16),
        ],
        after=[counted],
    )
    counted = next(rounds)
    attended, residual, normed2, turned, log_total = call(
        attend_kernel,
        (slots,),
        [
            (smem, lengths),
            (by_slot, patches),
            (by_window(3 * width), qkv),
            (whole(*w_out.shape), w_out),
            flat(bias_out),
            flat(norm2_gain),
            flat(norm2_bias),
        ],
        [
            (by_window(width), (total, width), bf16),
            (by_window(width), (total, width), f32),
            (by_window(width), (total, width), bf16),
            (pl.BlockSpec((width, rows), lambda i: (0, i)), (width, total), bf16),
            (by_head, (slots, 16, rows), f32),
        ],
        after=[counted],
    )
    for counted in rounds:
        pass
    window_total = jnp.sum(onehot * counted[None, :], axis=1)
    scales = jnp.where(live, 1.0 / jnp.maximum(window_total, 1.0), 0.0)

    by_lanes = pl.BlockSpec((total, width), lambda i: (0, i))
    up_spec = pl.BlockSpec((width, width), lambda i: (0, i))
    if fast:
        pair_share = hidden // parts
        pair_shape = (parts // 2, pair_share, width)
        pair_spec = pl.BlockSpec((parts // 2 // steps, pair_share, width), lambda i: (i, 0, 0))
        down_halves = [(pair_spec, pair_shape, f32)] * 2
    else:
        down_spec = pl.BlockSpec((width, width), lambda i: (i, 0))
        down_halves = [(down_spec, (hidden, width), f32), (whole(8, 128), (8, 128), f32)]
    activated, slope, grad_down, keep_down, send_down = call(
        mlp_kernel,
        (steps,),
        [
            (smem, lengths),
            (smem, scales),
            (smem, here),
            (whole(*cotangent.shape), cotangent),
            (whole(total, width), normed2),
            (up_spec, w_up),
            flat(bias_up.reshape(steps, width)),
        ],
        [
            (by_lanes, (total, hidden), bf16),
            (by_lanes, (total, hidden), bf16),
            (whole(total, width), (total, width), bf16),
        ]
        + down_halves,
    )
    if fast:
        shape = (parts // 2, share, hidden)
        up_halves = [(pl.BlockSpec((parts // 2, share, width), lambda i: (0, 0, i)), shape, f32)] * 2
    else:
        up_halves = [(up_spec, (width, hidden), f32), (whole(8, 128), (8, 128), f32)]
    grad_bias_up, grad_normed2, keep_up, send_up = call(
        mlp_back_kernel,
        (steps,),
        [
            (smem, here),
            (whole(total, width), grad_down),
            (by_lanes, slope),
            (whole(width, total), turned),
            (up_spec, w_up),
            (pl.BlockSpec((width, width), lambda i: (i, 0)), w_down),
        ],
        [
            (pl.BlockSpec((1, 1, width), lambda i: (i, 0, 0)), (steps, 1, width), f32),
            (whole(total, width), (total, width), f32),
        ]
        + up_halves,
    )

    def core_swap(send):
        return swap(send, "dp", 0) if fast else send

    def split_round(pairs, dims, parts, axes, after=(), carry=()):
        merge = len(set(axes)) == 1 and len({tuple(dims[p[0][0]]) for p in parts}) == 1
        gridded = all(d[0] == Z1 and len(d) > 1 for d in dims) and Z1 not in axes
        rows_here = pairs[0][0].shape[-2]
        blocks = 2 if gridded and rows_here % 48 == 0 else 1
        widths = [sum(width for _, _, width in part) for part in parts]
        left = [[d for d in dims[part[0][0]] if d != axis] for part, axis in zip(parts, axes)]
        if merge:
            widths, left = [sum(widths)], left[:1]
        shapes = [(2,) * len(d) + (rows_here, width) for d, width in zip(left, widths)]

        def spec(shape):
            if not gridded:
                return whole(*shape)
            block = (1,) + shape[1:-2] + (rows_here // blocks, shape[-1])
            return pl.BlockSpec(block, lambda i, j: (i,) + (0,) * (len(shape) - 3) + (j, 0))

        values = call(
            lambda *refs: split_kernel(dims, parts, axes, merge, gridded, *refs),
            (2, blocks) if gridded else (),
            [(smem, bits)] + [(spec(v.shape), v) for pair in pairs for v in pair],
            [(spec(shape), shape, f32) for shape in shapes for _ in range(2)],
            after=after,
            carry=carry,
        )
        states = [(values[2 * i], values[2 * i + 1]) for i in range(len(shapes))]
        return states, left, values[2 * len(shapes) :]

    class Chunk:
        def __init__(self, sources, orders, shares):
            self.sources, self.orders, self.step_count = sources, orders, 0
            self.columns = [[] for _ in orders]
            for i, cuts in enumerate(shares):
                start = 0
                for pieces, width in zip(self.columns, cuts):
                    pieces.append((i, start, width))
                    start += width

        def open(self, after=()):
            shaped = lambda v: v.reshape((2, 2, 2, 2, -1, v.shape[-1]))
            pairs = [(shaped(keep), shaped(come)) for keep, come in self.sources]
            axes = [order[0] for order in self.orders]
            dims = [[Z1, Z0, X, Y]] * len(pairs)
            self.put(split_round(pairs, dims, self.columns, axes, after), axes)

        def put(self, result, axes):
            self.states, self.dims, self.carried = result
            self.axes = axes[: len(self.states)]
            self.step_count += 1

        def pairs(self):
            return [
                (keep, swap(send, *LINKS[axis]))
                for (send, keep), axis in zip(self.states, self.axes)
            ]

        def step(self, after=(), carry=()):
            pairs = self.pairs()
            axes = [order[self.step_count] for order in self.orders][: len(pairs)]
            parts = [[(i, 0, keep.shape[-1])] for i, (keep, _) in enumerate(pairs)]
            self.put(split_round(pairs, self.dims, parts, axes, after, carry), axes)

        def finish(self, outputs):
            ((keep, come),) = self.pairs()
            own = keep + come
            other = swap(own, *LINKS[Y])
            moves, start = [], 0
            for pieces in self.columns:
                for source, first, wide in pieces:
                    for out, (origin, low, size) in enumerate(outputs):
                        begin, end = max(first, low), min(first + wide, low + size)
                        if origin == source and begin < end:
                            moves.append((out, begin - low, start + begin - first, end - begin))
                    start += wide
            shapes = [(2 * own.shape[0], size) for _, _, size in outputs]
            return call(
                lambda *refs: place_kernel(moves, *refs),
                (),
                [(smem, bits), (whole(*own.shape), own), (whole(*other.shape), other)],
                [(whole(*shape), shape, f32) for shape in shapes],
            )

        def tokens(self):
            return [value for state in self.states for value in state]

    come_down = core_swap(send_down)
    come_up = core_swap(send_up)
    two_orders = [(X, Y, Z0, Z1), (Y, X, Z0, Z1)]
    orders = [(X, Y, Z0, Z1), (Y, Z0, X, Z1), (Z0, X, Y, Z1)]
    tokens = []
    if fast:
        down = Chunk([(keep_down, come_down)], two_orders, [(width // 2,) * 2])
        down.open([grad_normed2])
        tokens = down.tokens()
    head_rows = (
        jnp.arange(16, dtype=jnp.int32)[:, None]
        == jnp.arange(width, dtype=jnp.int32)[None, :] // (width // HEADS)
    ).astype(bf16)
    grad_residual, grad_attended, delta, sums, branch_low = call(
        middle_back_kernel,
        (slots,),
        [
            (smem, lengths),
            (smem, scales),
            (smem, here),
            (by_slot, cotangent),
            (by_window(width), residual),
            (by_window(width), grad_normed2),
            (by_window(width), attended),
            (whole(*w_out.shape), w_out),
            flat(norm2_gain),
            (whole(*head_rows.shape), head_rows),
        ],
        [
            (by_window(width), (total, width), f32),
            (by_window(width), (total, width), bf16),
            (by_head, (slots, 16, rows), f32),
            (whole(8, width), (8, width), f32),
            (by_window(width), (total, width), bf16),
        ],
        after=tokens,
    )
    tokens = []
    if fast:
        up = Chunk(
            [(keep_up, come_up)], [(Z0, X, Y, Z1), (X, Z0, Y, Z1)], [(hidden // 2,) * 2]
        )
        up.open([grad_residual])
        tokens = up.tokens()

    grad_projected, bias_sums, keep_qkvo, send_qkvo = call(
        attend_back_kernel,
        (slots,),
        [
            (smem, lengths),
            (smem, here),
            (by_window(width, 0), qkv),
            (by_window(width, 1), qkv),
            (by_window(width, 2), qkv),
            (by_window(width), grad_attended),
            (by_window(width), normed),
            (by_head, log_total),
            (by_head, delta),
            (by_window(width), attended),
            (by_window(width), branch_low),
        ],
        [
            (by_window(3 * width), (total, 3 * width), bf16),
            (whole(8, width), (8, width), f32),
        ]
        + halves(parts // 2, 4 * width),
        [pltpu.VMEM((width, 4 * width), f32)],
        after=tokens,
    )
    come_qkvo = core_swap(send_qkvo)
    tokens = []
    if fast:
        down.step([grad_projected])
        up.step(down.tokens())
        tokens = up.tokens()
    grad_patches, late_sums, grad_leads = call(
        norm_back_kernel,
        (slots,),
        [
            (smem, leads),
            (by_slot, patches),
            (by_window(width), grad_residual),
            (by_window(3 * width), grad_projected),
            (whole(*w_qkv.shape), w_qkv),
            flat(norm1_gain),
        ],
        [
            (by_slot, patches.shape, bf16),
            (whole(8, width), (8, width), f32),
            (whole(lead_count, width), (lead_count, width), f32),
        ],
        after=tokens,
        micros=NB,
    )
    tokens = []
    if fast:
        last = Chunk([(keep_qkvo, come_qkvo)], orders, [LAST_SHARES])
        last.open([late_sums])
        down.step(last.tokens())
        up.step(down.tokens())
        tokens = up.tokens()

    (block_out,) = call(
        block_out_kernel,
        (slots,),
        [
            (by_window(hidden), activated),
            (whole(*w_down.shape), w_down),
            flat(bias_down),
            (by_window(width), residual),
        ],
        [(by_slot, patches.shape, bf16)],
        after=tokens,
    )

    bias_rows = grad_bias_up[:, 0]
    small = sum_small(jnp.concatenate([sums, bias_sums, late_sums, bias_rows, grad_leads], axis=0))
    up_rows = bias_rows.shape[0]

    if fast:
        down.step([block_out])
        last.step(down.tokens())
        up.step(last.tokens())
        (sum_down,) = down.finish([(0, 0, width)])
        last.step(up.tokens())
        last.step()
        (sum_up,) = up.finish([(0, 0, hidden)])
        sum_qkv, sum_out = last.finish([(0, 0, 3 * width), (0, 3 * width, width)])
    else:
        sum_down = scatter_sum(keep_down)
        sum_up = scatter_sum(keep_up)
        joined = scatter_sum(keep_qkvo)
        sum_qkv, sum_out = joined[:, : 3 * width], joined[:, 3 * width :]
    return (
        block_out,
        grad_patches,
        small[16],
        small[17],
        small[24 + up_rows :],
        sum_qkv,
        small[8],
        small[9],
        sum_out,
        small[2],
        small[0],
        small[1],
        sum_up,
        small[24 : 24 + up_rows].reshape(-1),
        sum_down,
        small[3],
    )


def solution(mesh):
    split = P(("dp", "outer"))
    placed = (split,) * 5 + (P(),) * 14
    row = P("dp", None)
    outs = (split, split, P(), P(), P(), row, P(), P(), row, P(), P(), P(), row, P(), row, P())
    return jax.shard_map(
        per_device, mesh=mesh, in_specs=placed, out_specs=outs, check_vma=False
    )
```

```python
import jax
import jax.numpy as jnp
from jax import lax
from jax.experimental import pallas as pl
from jax.experimental.pallas import tpu as pltpu
from jax.sharding import PartitionSpec as P

HEADS = 12
FORWARD_GROUP, BACK_GROUP = 2, 2
LEADS_AT = 16
SMALL_COLUMNS = 256
LAST_SHARES = (1024, 1024, 1024)
SEQUENCE = (
    "DO", "M", "UO", "A0", "D2", "A1", "U2", "D3", "QO", "U3", "NB", "D4", "BO", "U4", "Q2",
    "DA", "Q3", "DP", "UA", "Q4", "SX", "SZ", "QA", "UP", "SO", "QP",
)
PLAIN = ("M", "A0", "A1", "NB", "BO")
SMALL_NAMES = ("gain1", "bias1", "query", "value", "out", "gain2", "bias2", "down", "up", "table")
OUTPUTS = ("block_out", "grad_patches", "gain1", "bias1", "table", "sum_qkv", "query", "value")
OUTPUTS += ("sum_out", "out", "gain2", "bias2", "sum_up", "up", "sum_down", "down")
COSTS = {"D3": 100, "DO": 30, "A1": 2}
VMEM_BYTES = 63 * 1024 * 1024


norm_epsilon = 1e-05
masked_score = -1e30

density_scale = 0.3989422804014327


def dot_nn(a, b):
    return lax.dot_general(a, b, (((1,), (0,)), ((), ())), preferred_element_type=jnp.float32)


def dot_nt(a, b):
    return lax.dot_general(a, b, (((1,), (1,)), ((), ())), preferred_element_type=jnp.float32)


def dot_tn(a, b):
    return lax.dot_general(a, b, (((0,), (0,)), ((), ())), preferred_element_type=jnp.float32)


def normalise(values):
    centre = jnp.mean(values, axis=-1, keepdims=True)
    centred = values - centre
    spread = jnp.mean(centred * centred, axis=-1, keepdims=True)
    inverse = lax.rsqrt(spread + norm_epsilon)
    return centred * inverse, inverse


def normalise_back(grad, unit, inverse):
    first = jnp.mean(grad, axis=-1, keepdims=True)
    second = jnp.mean(grad * unit, axis=-1, keepdims=True)
    return inverse * (grad - first - unit * second)


def column_sum(values):
    return jnp.sum(values, axis=0, keepdims=True)


def gelu_pair(pre):
    normal = 0.5 + 0.5 * lax.erf(pre * 0.7071067811865476)
    return pre * normal, normal + pre * (density_scale * jnp.exp(-0.5 * (pre * pre)))


def line(vector):
    return vector[...].reshape(1, -1)


def project_kernel(
    leads, patches, gain, bias, bias_query, bias_value, lead_table, w_qkv, normed, qkv
):
    window = pl.program_id(0)
    width = patches.shape[-1]
    unit, _ = normalise(patches[0].astype(jnp.float32))
    lead_row = lead_table[pl.ds(leads[window], 1), :]
    low = (unit * line(gain) + line(bias) + lead_row).astype(jnp.bfloat16)
    normed[...] = low
    queries = dot_nn(low, w_qkv[:, :width]) + line(bias_query)
    qkv[:, :width] = queries.astype(jnp.bfloat16) * 0.125
    qkv[:, width : 2 * width] = dot_nn(low, w_qkv[:, width : 2 * width]).astype(jnp.bfloat16)
    values = dot_nn(low, w_qkv[:, 2 * width :]) + line(bias_value)
    qkv[:, 2 * width :] = values.astype(jnp.bfloat16)


def each_alone(columns, place):
    zero = jnp.zeros_like(columns)
    return jnp.concatenate([jnp.where(place == i, columns, zero) for i in range(columns.shape[1] // 64)], axis=0)


def own_columns(stacked, place):
    rows = place.shape[0]
    joined = stacked[:rows]
    for i in range(1, stacked.shape[1] // 64):
        joined = jnp.where(place == i, stacked[i * rows : (i + 1) * rows], joined)
    return joined


def attend_kernel(
    lengths,
    patches,
    qkv,
    w_out,
    bias_out,
    gain,
    bias,
    attended,
    residual,
    normed2,
    turned,
    log_total,
):
    window = pl.program_id(0)
    _, rows, width = patches.shape
    keys_at = lax.broadcasted_iota(jnp.int32, (rows, 1), 0)
    blocked = jnp.where(keys_at < lengths[window], 0.0, masked_score)
    span = FORWARD_GROUP * 64
    place = lax.broadcasted_iota(jnp.int32, (rows, span), 1) // 64
    for at in range(0, width, span):
        query = each_alone(qkv[:, at : at + span], place)
        key = qkv[:, width + at : width + at + span]
        value = qkv[:, 2 * width + at : 2 * width + at + span]
        scores = dot_nt(key, query) + blocked
        top = jnp.max(scores, axis=0, keepdims=True)
        exponent = jnp.exp(scores - top)
        total = jnp.sum(exponent, axis=0, keepdims=True)
        probs = (exponent * (1.0 / total)).astype(jnp.bfloat16)
        out = own_columns(dot_tn(probs, value), place)
        attended[:, at : at + span] = out.astype(jnp.bfloat16)
        log_sum = top + jnp.log(total)
        for i in range(FORWARD_GROUP):
            head = at // 64 + i
            log_total[0, head : head + 1, :] = log_sum[:, i * rows : (i + 1) * rows]
    branch = dot_nn(attended[...], w_out[...]) + line(bias_out)
    held = patches[0].astype(jnp.float32) + branch
    residual[...] = held
    unit, _ = normalise(held)
    low = (unit * line(gain) + line(bias)).astype(jnp.bfloat16)
    normed2[...] = low
    turned[...] = low.T


def store_halves(result, here, keep, send):
    if keep.ndim == 2:
        keep[...] = result
        send[...] = jnp.zeros_like(send)
        return
    blocks, share, columns = keep.shape
    split = result.reshape(blocks, 2, share, columns)
    first, second = split[:, 0], split[:, 1]
    keep[...] = jnp.where(here == 0, first, second)
    send[...] = jnp.where(here == 0, second, first)


def mlp_kernel(
    lengths,
    scales,
    here,
    cotangent,
    normed2,
    w_up,
    bias_up,
    activated,
    slope,
    grad_down,
    keep,
    send,
):
    windows, rows, width = cotangent.shape
    step = pl.program_id(0)

    @pl.when(step == 0)
    def _():
        row = lax.broadcasted_iota(jnp.int32, (rows, 1), 0)
        for window in range(windows):
            weight = jnp.where(row < lengths[window], scales[window], 0.0)
            grad = (cotangent[window].astype(jnp.float32) * weight).astype(jnp.bfloat16)
            grad_down[window * rows : (window + 1) * rows, :] = grad

    bias = bias_up[pl.ds(pl.multiple_of(step * width, 128), width)]
    for window in range(windows):
        at = slice(window * rows, (window + 1) * rows)
        pre = dot_nn(normed2[at, :], w_up[...]) + bias.reshape(1, -1)
        out, steep = gelu_pair(pre)
        out = out.astype(jnp.bfloat16)
        activated[at, :] = out
        slope[at, :] = steep.astype(jnp.bfloat16)
    store_halves(dot_tn(activated[...], grad_down[...]), here[0], keep, send)


def mlp_back_kernel(
    here, grad_down, slope, turned, w_up, w_down, grad_bias_up, grad_normed2, keep, send
):
    step = pl.program_id(0)

    @pl.when(step == 0)
    def _():
        grad_normed2[...] = jnp.zeros_like(grad_normed2)

    grad_act = dot_nt(grad_down[...], w_down[...])
    grad_up = (grad_act * slope[...].astype(jnp.float32)).astype(jnp.bfloat16)
    grad_bias_up[0] = column_sum(grad_up.astype(jnp.float32))
    store_halves(dot_nn(turned[...], grad_up), here[0], keep, send)
    grad_normed2[...] += dot_nt(grad_up, w_up[...])


def middle_back_kernel(
    lengths,
    scales,
    here,
    cotangent,
    residual,
    grad_normed2,
    attended,
    w_out,
    gain,
    head_rows,
    grad_residual,
    grad_attended,
    delta,
    sums,
    branch_low,
):
    window = pl.program_id(0)
    _, rows, width = cotangent.shape

    @pl.when(window == 0)
    def _():
        sums[...] = jnp.zeros_like(sums)

    row = lax.broadcasted_iota(jnp.int32, (rows, 1), 0)
    weight = jnp.where(row < lengths[window], scales[window], 0.0)
    grad_out = cotangent[0].astype(jnp.float32) * weight
    unit, inverse = normalise(residual[...])
    grad_norm = grad_normed2[...]
    held = grad_out + normalise_back(grad_norm * line(gain), unit, inverse)
    grad_residual[...] = held
    branch = held.astype(jnp.bfloat16)
    branch_low[...] = branch
    sums[0:1, :] += column_sum(grad_norm * unit)
    sums[1:2, :] += column_sum(grad_norm)
    sums[2:3, :] += column_sum(branch.astype(jnp.float32))
    sums[3:4, :] += column_sum(grad_out.astype(jnp.bfloat16).astype(jnp.float32))
    grad_att = dot_nt(branch, w_out[...]).astype(jnp.bfloat16)
    grad_attended[...] = grad_att
    product = grad_att.astype(jnp.float32) * attended[...].astype(jnp.float32)
    high = product.astype(jnp.bfloat16)
    low = (product - high.astype(jnp.float32)).astype(jnp.bfloat16)
    delta[0] = dot_nt(head_rows[...], high) + dot_nt(head_rows[...], low)


def attend_back_heads(first, lengths, refs, log_total, delta, out, columns):
    queries, keys, values, grad_attended = refs
    rows, width = queries.shape
    row = lax.broadcasted_iota(jnp.int32, (rows, 1), 0)
    blocked = jnp.where(row < lengths[pl.program_id(0)], 0.0, masked_score)
    span = BACK_GROUP * 64
    place = lax.broadcasted_iota(jnp.int32, (rows, span), 1) // 64

    def start(at):
        query = each_alone(queries[:, at : at + span], place)
        grad_group = each_alone(grad_attended[:, at : at + span], place)
        scores = dot_nt(keys[:, at : at + span], query) + blocked
        return query, grad_group, scores, dot_nt(values[:, at : at + span], grad_group)

    ahead = start(0)
    for at in range(0, width, span):
        query, grad_group, scores, grad_probs = ahead
        if at + span < width:
            ahead = start(at + span)
        heads = range(first + at // 64, first + at // 64 + BACK_GROUP)
        totals = jnp.concatenate([log_total[0, h : h + 1, :] for h in heads], axis=1)
        shift = jnp.concatenate([delta[0, h : h + 1, :] for h in heads], axis=1)
        probs = jnp.exp(scores - totals)
        grad_scores = (probs * (grad_probs - shift)).astype(jnp.bfloat16)
        grad_query = own_columns(dot_tn(grad_scores, keys[:, at : at + span]), place) * 0.125
        grad_key = dot_nn(grad_scores, query)
        grad_value = dot_nn(probs.astype(jnp.bfloat16), grad_group)
        for index, grad in enumerate((grad_query, grad_key, grad_value)):
            to = columns[index] + at
            out[:, to : to + span] = grad.astype(jnp.bfloat16)


def attend_back_first_kernel(lengths, queries, keys, values, grad_attended, log_total, delta, out):
    half = queries.shape[1]
    refs = (queries, keys, values, grad_attended)
    attend_back_heads(0, lengths, refs, log_total, delta, out, (0, half, 2 * half))


def attend_back_kernel(
    lengths,
    here,
    queries,
    keys,
    values,
    grad_attended,
    normed,
    log_total,
    delta,
    attended,
    branch,
    first,
    grad_projected,
    sums,
    keep,
    send,
    grad_w,
):
    window = pl.program_id(0)
    half = queries.shape[1]
    width = 2 * half

    @pl.when(window == 0)
    def _():
        grad_w[...] = jnp.zeros_like(grad_w)
        sums[...] = jnp.zeros_like(sums)

    refs = (queries, keys, values, grad_attended)
    columns = (half, width + half, 2 * width + half)
    attend_back_heads(HEADS // 2, lengths, refs, log_total, delta, grad_projected, columns)
    for third in range(3):
        part = first[:, third * half : (third + 1) * half]
        grad_projected[:, third * width : third * width + half] = part
    grad_w[:, : 3 * width] += dot_tn(normed[...], grad_projected[...])
    grad_w[:, 3 * width :] += dot_tn(attended[...], branch[...])
    sums[0:1, :] += column_sum(grad_projected[:, :width].astype(jnp.float32))
    sums[1:2, :] += column_sum(grad_projected[:, 2 * width :].astype(jnp.float32))

    @pl.when(window == pl.num_programs(0) - 1)
    def _():
        store_halves(grad_w[...], here[0], keep, send)


def norm_back_kernel(
    leads,
    patches,
    grad_residual,
    grad_projected,
    w_qkv,
    gain,
    middle_sums,
    bias_sums,
    bias_rows,
    grad_patches,
    small,
):
    window = pl.program_id(0)

    def put(row, value, add=False):
        for piece in range(value.shape[1] // SMALL_COLUMNS):
            at = pl.ds(row * (value.shape[1] // SMALL_COLUMNS) + piece, 1)
            part = value[:, piece * SMALL_COLUMNS : (piece + 1) * SMALL_COLUMNS]
            small[at, :] = small[at, :] + part if add else part

    @pl.when(window == 0)
    def _():
        small[...] = jnp.zeros_like(small)
        for row in range(4):
            put(row, middle_sums[row : row + 1, :])
        for row in range(2):
            put(4 + row, bias_sums[row : row + 1, :])
        for row in range(bias_rows.shape[0]):
            put(8 + row, bias_rows[row])

    grad_norm = dot_nt(grad_projected[...], w_qkv[...])
    unit, inverse = normalise(patches[0].astype(jnp.float32))
    back = normalise_back(grad_norm * line(gain), unit, inverse)
    grad_patches[0] = (grad_residual[...] + back).astype(jnp.bfloat16)
    total = column_sum(grad_norm)
    put(6, column_sum(grad_norm * unit), add=True)
    put(7, total, add=True)
    put(LEADS_AT + leads[window], total, add=True)


def block_out_kernel(activated, w_down, bias_down, residual, block_out):
    final = residual[...] + dot_nn(activated[...], w_down[...]) + line(bias_down)
    block_out[0] = final.astype(jnp.bfloat16)


Z1, Z0, X, Y = range(4)
LINKS = (("dp", 3), ("dp", 2), ("dp", 1), ("outer", 0))


def split_kernel(pairs, parts, axes, merge, gridded, riders, bits, *refs):
    outs = refs[2 * len(pairs) + (riders == "join") :]
    start = 0
    for index, (pieces, axis) in enumerate(zip(parts, axes)):
        send, keep = outs[:2] if merge else outs[2 * index : 2 * index + 2]
        if not merge:
            start = 0
        mine = bits[axis]
        for pair, first, width in pieces:
            held, come = refs[2 * pair], refs[2 * pair + 1]
            at = [slice(None)] * len(held.shape)
            if gridded:
                at[0] = 0
            at[-1] = slice(first, first + width)
            place = pairs[pair].index(axis)
            for out, side in ((send, 1 - mine), (keep, mine)):
                at[place] = side
                value = held[tuple(at)] + come[tuple(at)]
                to = (Ellipsis, slice(start, start + width))
                out[(0,) + to if gridded else to] = value
            start += width
    if riders == "join":
        rider = refs[2 * len(pairs)]
        rows, wide = outs[0].shape[0], rider.shape[1]
        for out in outs[:2]:
            for side in range(2):
                to = slice(start + side * wide, start + (side + 1) * wide)
                out[:, to] = rider[side * rows : (side + 1) * rows, :]


def add_kernel(held, come, out):
    out[...] = held[...] + come[...]


SMALL_ROWS = (6, 7, 4, 5, 2, 0, 1, 3)


def small_out_kernel(held, come, *outs):
    total = held[...] + come[...]
    columns = total.shape[1]
    vectors, bias_up, table = outs[:8], outs[8], outs[9]
    pieces = table.shape[1] // columns

    def copy(row, out, start):
        for piece in range(pieces):
            value = total[row * pieces + piece : row * pieces + piece + 1, :]
            out[pl.ds(start + piece * columns, columns)] = value.reshape(columns)

    for row, out in zip(SMALL_ROWS, vectors):
        copy(row, out, 0)
    for row in range(bias_up.shape[0] // table.shape[1]):
        copy(8 + row, bias_up, row * table.shape[1])
    for row in range(table.shape[0]):
        for piece in range(pieces):
            at = (LEADS_AT + row) * pieces + piece
            table[row : row + 1, piece * columns : (piece + 1) * columns] = total[at : at + 1, :]


def place_kernel(moves, rider, bits, own, other, *outs):
    rows = own.shape[0]
    mine = bits[Y]
    for out, to, start, width in moves:
        for value, side in ((own, mine), (other, 1 - mine)):
            outs[out][pl.ds(side * rows, rows), to : to + width] = value[:, start : start + width]
    if rider is not None:
        wide = outs[-1].shape[1]
        for side in range(2):
            at = slice(rider + side * wide, rider + (side + 1) * wide)
            outs[-1][side * rows : (side + 1) * rows, :] = own[:, at] + other[:, at]


DOWN_ORDERS, DOWN_SHARES = [(X, Y, Z0, Z1), (Y, X, Z0, Z1)], (384, 384)
UP_ORDERS, UP_SHARES = [(Z0, X, Y, Z1), (X, Z0, Y, Z1)], (1920, 1152)
LAST_ORDERS = [(X, Y, Z0, Z1), (Y, Z0, X, Z1), (Z0, X, Y, Z1)]


def swap(values, axis, bit):
    size = lax.axis_size(axis)
    return lax.ppermute(values, axis, [(i, i ^ (1 << bit)) for i in range(size)])


def bit_of(axis, bit):
    return lax.rem(lax.div(lax.axis_index(axis), 1 << bit), 2)


def dp_bits():
    return lax.axis_size("dp").bit_length() - 1


def exchange(values, dp_mask, outer_mask):
    inner = lax.axis_size("outer")
    size = lax.axis_size("dp") * inner
    flip = dp_mask * inner + outer_mask
    return lax.ppermute(values, ("dp", "outer"), [(i, i ^ flip) for i in range(size)])


def count_rounds(values):
    steps = [(1 << bit, 0) for bit in range(1, dp_bits())] + [(0, 1)]
    rounds = [[(1, 0)]] + [steps[at : at + 2] for at in range(0, len(steps), 2)]
    for group in rounds:
        flips = list(group)
        if len(group) == 2:
            flips.append((group[0][0] | group[1][0], group[0][1] | group[1][1]))
        values = values + sum(exchange(values, *flip) for flip in flips)
        yield values


def part_orders(bit_count):
    rest = list(range(3, bit_count))
    return (
        [("dp", 1), ("outer", 0), ("dp", 2)] + [("dp", b) for b in rest],
        [("outer", 0), ("dp", 2), ("dp", 1)] + [("dp", b) for b in rest],
        [("dp", 2), ("dp", 1), ("outer", 0)] + [("dp", b) for b in rest],
    )


def halve(values, dims, step):
    axis, bit = step
    place = dims.index(step)
    mine = bit_of(axis, bit)
    keep = lax.dynamic_index_in_dim(values, mine, place, keepdims=False)
    send = lax.dynamic_index_in_dim(values, 1 - mine, place, keepdims=False)
    left = dims[:place] + dims[place + 1 :]
    return keep + swap(send, axis, bit), left


def scatter_sum(matrix):
    bit_count = dp_bits()
    rows, columns = matrix.shape
    share = rows // lax.axis_size("dp")
    dims = [("dp", b) for b in range(bit_count - 1, -1, -1)] + [("outer", 0)]
    values = matrix.reshape((2,) * bit_count + (2, share // 2, columns))
    values, dims = halve(values, dims, ("dp", 0))
    third = columns // 3
    pieces = []
    for index, order in enumerate(part_orders(bit_count)):
        part = lax.slice_in_dim(values, index * third, (index + 1) * third, axis=values.ndim - 1)
        left = dims
        for step in order:
            part, left = halve(part, left, step)
        pieces.append(part)
    mine = jnp.concatenate(pieces, axis=1)
    other = swap(mine, "outer", 0)
    first = lax.axis_index("outer") == 0
    return jnp.concatenate([jnp.where(first, mine, other), jnp.where(first, other, mine)], axis=0)


def per_device(
    patches,
    lengths,
    leads,
    counts,
    cotangent,
    norm1_gain,
    norm1_bias,
    lead_table,
    w_qkv,
    bias_query,
    bias_value,
    w_out,
    bias_out,
    norm2_gain,
    norm2_bias,
    w_up,
    bias_up,
    w_down,
    bias_down,
):
    slots, rows, width = patches.shape
    total = slots * rows
    hidden = w_up.shape[1]
    lead_count = lead_table.shape[0]
    steps = hidden // width
    f32, bf16 = jnp.float32, jnp.bfloat16
    parts = lax.axis_size("dp")
    share = width // parts
    fast = parts == 16 and share % 16 == 0 and slots == 4

    smem = pl.BlockSpec(memory_space=pltpu.SMEM)
    params = pltpu.CompilerParams(vmem_limit_bytes=VMEM_BYTES)

    def whole(*shape):
        return pl.BlockSpec(shape, lambda *i: (0,) * len(shape))

    def by_window(columns, at=0):
        return pl.BlockSpec((rows, columns), lambda i: (i, at))

    current = [""]

    def call(kernel, grid, inputs, outs, scratch=(), after=(), carry=()):
        count, extra, carried = len(inputs), len(after) + len(carry), len(carry)
        made = count + extra + len(outs)

        def body(*refs):
            kernel(*refs[:count], *refs[count + extra : made], *refs[made + carried :])

        anywhere = pl.BlockSpec(memory_space=pl.ANY)
        return pl.pallas_call(
            body,
            grid=grid,
            in_specs=[spec for spec, _ in inputs] + [anywhere] * extra,
            out_specs=[spec for spec, _, _ in outs] + [anywhere] * carried,
            out_shape=[jax.ShapeDtypeStruct(shape, dtype) for _, shape, dtype in outs]
            + [jax.ShapeDtypeStruct(value.shape, value.dtype) for value in carry],
            input_output_aliases={
                count + len(after) + i: len(outs) + i for i in range(carried)
            },
            scratch_shapes=scratch,
            compiler_params=params,
            cost_estimate=pl.CostEstimate(
                flops=int(COSTS.get(current[0], 0) * 1.15e9), bytes_accessed=0, transcendentals=0
            ),
        )(*[value for _, value in inputs], *after, *carry)

    live = jnp.arange(slots, dtype=jnp.int32) < counts[0]
    onehot = (leads[:, None] == jnp.arange(lead_count, dtype=jnp.int32)[None, :]).astype(f32)
    rounds = count_rounds(jnp.sum(onehot * live[:, None].astype(f32), axis=0))
    counted = next(rounds)

    dp_at, outer_at = lax.axis_index("dp"), lax.axis_index("outer")
    here = lax.rem(dp_at, 2).reshape(1)
    bits = jnp.stack([bit_of("dp", 3), bit_of("dp", 2), bit_of("dp", 1), outer_at])
    def flat(vector):
        return whole(*vector.shape), vector

    by_slot = pl.BlockSpec((1, rows, width), lambda i: (i, 0, 0))
    by_head = pl.BlockSpec((1, 16, rows), lambda i: (i, 0, 0))

    def halves(blocks, columns, grid_axis=None):
        if not fast:
            spec = pl.BlockSpec((width, columns), lambda i: (0, 0))
            return [(spec, (width, columns), f32), (whole(8, 128), (8, 128), f32)]
        shape = (parts // 2, share, columns)
        return [(whole(*shape), shape, f32)] * 2

    normed, qkv = call(
        project_kernel,
        (slots,),
        [
            (smem, leads),
            (by_slot, patches),
            flat(norm1_gain),
            flat(norm1_bias),
            flat(bias_query),
            flat(bias_value),
            (whole(*lead_table.shape), lead_table),
            (whole(*w_qkv.shape), w_qkv),
        ],
        [
            (by_window(width), (total, width), bf16),
            (by_window(3 * width), (total, 3 * width), bf16),
        ],
        after=[counted],
    )
    counted = next(rounds)
    attended, residual, normed2, turned, log_total = call(
        attend_kernel,
        (slots,),
        [
            (smem, lengths),
            (by_slot, patches),
            (by_window(3 * width), qkv),
            (whole(*w_out.shape), w_out),
            flat(bias_out),
            flat(norm2_gain),
            flat(norm2_bias),
        ],
        [
            (by_window(width), (total, width), bf16),
            (by_window(width), (total, width), f32),
            (by_window(width), (total, width), bf16),
            (pl.BlockSpec((width, rows), lambda i: (0, i)), (width, total), bf16),
            (by_head, (slots, 16, rows), f32),
        ],
        after=[counted],
    )
    for counted in rounds:
        pass
    window_total = jnp.sum(onehot * counted[None, :], axis=1)
    scales = jnp.where(live, 1.0 / jnp.maximum(window_total, 1.0), 0.0)

    by_lanes = pl.BlockSpec((total, width), lambda i: (0, i))
    up_spec = pl.BlockSpec((width, width), lambda i: (0, i))
    if fast:
        pair_share = hidden // parts
        pair_shape = (parts // 2, pair_share, width)
        pair_spec = pl.BlockSpec((parts // 2 // steps, pair_share, width), lambda i: (i, 0, 0))
        down_halves = [(pair_spec, pair_shape, f32)] * 2
    else:
        down_spec = pl.BlockSpec((width, width), lambda i: (i, 0))
        down_halves = [(down_spec, (hidden, width), f32), (whole(8, 128), (8, 128), f32)]
    activated, slope, grad_down, keep_down, send_down = call(
        mlp_kernel,
        (steps,),
        [
            (smem, lengths),
            (smem, scales),
            (smem, here),
            (whole(*cotangent.shape), cotangent),
            (whole(total, width), normed2),
            (up_spec, w_up),
            flat(bias_up),
        ],
        [
            (by_lanes, (total, hidden), bf16),
            (by_lanes, (total, hidden), bf16),
            (whole(total, width), (total, width), bf16),
        ]
        + down_halves,
    )
    if fast:
        shape = (parts // 2, share, hidden)
        up_halves = [(pl.BlockSpec((parts // 2, share, width), lambda i: (0, 0, i)), shape, f32)] * 2
    else:
        up_halves = [(up_spec, (width, hidden), f32), (whole(8, 128), (8, 128), f32)]
    grad_bias_up, grad_normed2, keep_up, send_up = call(
        mlp_back_kernel,
        (steps,),
        [
            (smem, here),
            (whole(total, width), grad_down),
            (by_lanes, slope),
            (whole(width, total), turned),
            (up_spec, w_up),
            (pl.BlockSpec((width, width), lambda i: (i, 0)), w_down),
        ],
        [
            (pl.BlockSpec((1, 1, width), lambda i: (i, 0, 0)), (steps, 1, width), f32),
            (whole(total, width), (total, width), f32),
        ]
        + up_halves,
    )

    def core_swap(send):
        return swap(send, "dp", 0) if fast else send

    def split_round(pairs, dims, parts, axes, done, rider=None):
        riders = "join" if rider is not None else None
        merge = len(set(axes)) == 1 and len({tuple(dims[p[0][0]]) for p in parts}) == 1
        gridded = all(d[0] == Z1 and len(d) > 1 for d in dims) and Z1 not in axes and not riders
        rows_here = pairs[0][0].shape[-2]
        blocks = 2 if gridded and rows_here % 48 == 0 else 1
        widths = [sum(width for _, _, width in part) for part in parts]
        left = [[d for d in dims[part[0][0]] if d != axis] for part, axis in zip(parts, axes)]
        if merge:
            widths, left = [sum(widths)], left[:1]
            if riders == "join":
                widths = [widths[0] + 2 * rider.shape[-1]]
        shapes = [(2,) * len(d) + (rows_here, width) for d, width in zip(left, widths)]

        def spec(shape):
            if not gridded:
                return whole(*shape)
            block = (1,) + shape[1:-2] + (rows_here // blocks, shape[-1])
            middle = (0,) * (len(shape) - 3)
            return pl.BlockSpec(block, lambda i: (i // blocks, *middle, i % blocks, 0))

        inputs = [(smem, bits)] + [(spec(v.shape), v) for pair in pairs for v in pair]
        if riders == "join":
            inputs.append((spec(rider.shape), rider))
        outs = [(spec(shape), shape, f32) for shape in shapes for _ in range(2)]

        def kernel(*refs):
            split_kernel(dims, parts, axes, merge, gridded, riders, *refs)

        def finish(values):
            done([(values[2 * i], values[2 * i + 1]) for i in range(len(shapes))], left)
            return list(values)

        return kernel, (2 * blocks,) if gridded else (), inputs, outs, [], finish

    class Chunk:
        def __init__(self, sources, orders, shares):
            self.sources, self.orders, self.step_count = sources, orders, 0
            self.columns = [[] for _ in orders]
            for i, cuts in enumerate(shares):
                start = 0
                for pieces, width in zip(self.columns, cuts):
                    pieces.append((i, start, width))
                    start += width

        def open(self):
            shaped = lambda v: v.reshape((2, 2, 2, 2, -1, v.shape[-1]))
            pairs = [(shaped(keep), shaped(come)) for keep, come in self.sources]
            axes = [order[0] for order in self.orders]
            dims = [[Z1, Z0, X, Y]] * len(pairs)
            return split_round(pairs, dims, self.columns, axes, self.put)

        def put(self, states, dims):
            self.states, self.dims = states, dims
            self.axes = [order[self.step_count] for order in self.orders][: len(states)]
            self.step_count += 1

        def pairs(self):
            return [
                (keep, swap(send, *LINKS[axis]))
                for (send, keep), axis in zip(self.states, self.axes)
            ]

        def step(self, rider=None):
            pairs = self.pairs()
            axes = [order[self.step_count] for order in self.orders][: len(pairs)]
            parts = [[(i, 0, keep.shape[-1])] for i, (keep, _) in enumerate(pairs)]
            return split_round(pairs, self.dims, parts, axes, self.put, rider)

        def add(self):
            ((keep, come),) = self.pairs()
            spec = whole(*keep.shape)

            def finish(values):
                (self.own,) = values
                return values

            inputs = [(spec, keep), (spec, come)]
            return add_kernel, (), inputs, [(spec, keep.shape, f32)], [], finish

        def place(self, outputs, finish, rider=False):
            own = self.own
            other = swap(own, *LINKS[Y])
            moves, start = [], 0
            for pieces in self.columns:
                for source, first, wide in pieces:
                    for out, (origin, low, size) in enumerate(outputs):
                        begin, end = max(first, low), min(first + wide, low + size)
                        if origin == source and begin < end:
                            moves.append((out, begin - low, start + begin - first, end - begin))
                    start += wide
            shapes = [(2 * own.shape[0], size) for _, _, size in outputs]
            if rider:
                shapes.append((2 * own.shape[0], (own.shape[1] - start) // 2))

            def kernel(*refs):
                place_kernel(moves, start if rider else None, *refs)

            inputs = [(smem, bits), (whole(*own.shape), own), (whole(*other.shape), other)]
            outs = [(whole(*shape), shape, f32) for shape in shapes]
            return kernel, (), inputs, outs, [], finish

    come_down = core_swap(send_down)
    come_up = core_swap(send_up)
    head_rows = (
        jnp.arange(16, dtype=jnp.int32)[:, None]
        == jnp.arange(width, dtype=jnp.int32)[None, :] // (width // HEADS)
    ).astype(bf16)
    made = {}

    def keep_results(*names):
        def finish(values):
            made.update(zip(names, values))
            return list(values[:1])

        return finish

    def middle():
        return (
            middle_back_kernel,
            (slots,),
            [
                (smem, lengths),
                (smem, scales),
                (smem, here),
                (by_slot, cotangent),
                (by_window(width), residual),
                (by_window(width), grad_normed2),
                (by_window(width), attended),
                (whole(*w_out.shape), w_out),
                flat(norm2_gain),
                (whole(*head_rows.shape), head_rows),
            ],
            [
                (by_window(width), (total, width), f32),
                (by_window(width), (total, width), bf16),
                (by_head, (slots, 16, rows), f32),
                (whole(8, width), (8, width), f32),
                (by_window(width), (total, width), bf16),
            ],
            [],
            keep_results("grad_residual", "grad_attended", "delta", "sums", "branch"),
        )

    half = width // 2

    def attention_first():
        return (
            attend_back_first_kernel,
            (slots,),
            [
                (smem, lengths),
                (by_window(half, 0), qkv),
                (by_window(half, 2), qkv),
                (by_window(half, 4), qkv),
                (by_window(half, 0), made["grad_attended"]),
                (by_head, log_total),
                (by_head, made["delta"]),
            ],
            [(by_window(3 * half), (total, 3 * half), bf16)],
            [],
            keep_results("projected_first"),
        )

    def attention():
        return (
            attend_back_kernel,
            (slots,),
            [
                (smem, lengths),
                (smem, here),
                (by_window(half, 1), qkv),
                (by_window(half, 3), qkv),
                (by_window(half, 5), qkv),
                (by_window(half, 1), made["grad_attended"]),
                (by_window(width), normed),
                (by_head, log_total),
                (by_head, made["delta"]),
                (by_window(width), attended),
                (by_window(width), made["branch"]),
                (by_window(3 * half), made["projected_first"]),
            ],
            [
                (by_window(3 * width), (total, 3 * width), bf16),
                (whole(8, width), (8, width), f32),
            ]
            + halves(parts // 2, 4 * width),
            [pltpu.VMEM((width, 4 * width), f32)],
            keep_results("grad_projected", "bias_sums", "keep_last", "send_last"),
        )

    def first_norm():
        small_rows = 64 * width // SMALL_COLUMNS
        return (
            norm_back_kernel,
            (slots,),
            [
                (smem, leads),
                (by_slot, patches),
                (by_window(width), made["grad_residual"]),
                (by_window(3 * width), made["grad_projected"]),
                (whole(*w_qkv.shape), w_qkv),
                flat(norm1_gain),
                (whole(*made["sums"].shape), made["sums"]),
                (whole(*made["bias_sums"].shape), made["bias_sums"]),
                (whole(*grad_bias_up.shape), grad_bias_up),
            ],
            [
                (by_slot, patches.shape, bf16),
                (whole(small_rows, SMALL_COLUMNS), (small_rows, SMALL_COLUMNS), f32),
            ],
            [],
            keep_results("grad_patches", "small"),
        )

    def output():
        return (
            block_out_kernel,
            (slots,),
            [
                (by_window(hidden), activated),
                (whole(*w_down.shape), w_down),
                flat(bias_down),
                (by_window(width), residual),
            ],
            [(by_slot, patches.shape, bf16)],
            [],
            keep_results("block_out"),
        )

    def add_small(bit):
        small = made["small"]
        spec = whole(*small.shape)
        inputs = [(spec, small), (spec, swap(small, "dp", bit))]
        return add_kernel, (), inputs, [(spec, small.shape, f32)], [], keep_results("small")

    def small_outs():
        small = made["small"]
        spec = whole(*small.shape)
        shapes = [(width,)] * 8 + [bias_up.shape, lead_table.shape]
        outs = [(whole(*shape), shape, f32) for shape in shapes]
        inputs = [(spec, small), (spec, swap(small, "dp", 0))]
        return small_out_kernel, (), inputs, outs, [], keep_results(*SMALL_NAMES)

    def run(works, after):
        counts = [[len(work[part]) for work in works] for part in (2, 3, 4)]

        def kernel(*refs):
            at = 0
            groups = [[] for _ in works]
            for part in counts:
                for group, count in zip(groups, part):
                    group.extend(refs[at : at + count])
                    at += count
            for work, group in zip(works, groups):
                work[0](*group)

        joined = [[item for work in works for item in work[part]] for part in (2, 3, 4)]
        values = call(kernel, works[0][1], *joined, after=after)
        tokens, at = [], 0
        for work, count in zip(works, counts[1]):
            tokens += work[5](values[at : at + count])
            at += count
        return tokens

    def build(event):
        name, step = event[0], event[1:]
        if event in PLAIN:
            works = (middle, attention_first, attention, first_norm, output)
            return works[PLAIN.index(event)]()
        if name == "S":
            return small_outs() if step == "O" else add_small({"X": 1, "Z": 2}[step])
        if step == "O":
            keep, send, orders, shares = {
                "D": (keep_down, send_down, DOWN_ORDERS, DOWN_SHARES),
                "U": (keep_up, send_up, UP_ORDERS, UP_SHARES),
                "Q": (made.get("keep_last"), made.get("send_last"), LAST_ORDERS, LAST_SHARES),
            }[name]
            chunks[name] = Chunk([(keep, core_swap(send))], orders, [shares])
            return chunks[name].open()
        chunk = chunks[name]
        if step == "A":
            return chunk.add()
        if event == "DP":
            return chunk.place([(0, 0, width)], keep_results("sum_down", "small"), rider=True)
        if event == "UP":
            return chunk.place([(0, 0, hidden)], keep_results("sum_up"))
        if event == "QP":
            outputs = [(0, 0, 3 * width), (0, 3 * width, width)]
            return chunk.place(outputs, keep_results("sum_qkv", "sum_out"))
        return chunk.step(made["small"] if event == "D4" else None)

    chunks = {}
    tokens = [grad_normed2]
    for group in SEQUENCE if fast else PLAIN:
        current[0] = group
        tokens = run([build(event) for event in group.split("+")], tokens)
    if not fast:
        for bit in range(1, dp_bits()):
            made["small"] = made["small"] + swap(made["small"], "dp", bit)
        made["small"] = made["small"] + swap(made["small"], "outer", 0)
        run([small_outs()], ())
        made["sum_down"] = scatter_sum(keep_down)
        made["sum_up"] = scatter_sum(keep_up)
        joined = scatter_sum(made["keep_last"])
        made["sum_qkv"], made["sum_out"] = joined[:, : 3 * width], joined[:, 3 * width :]
    return tuple(made[name] for name in OUTPUTS)


def solution(mesh):
    split = P(("dp", "outer"))
    placed = (split,) * 5 + (P(),) * 14
    row = P("dp", None)
    outs = (split, split, P(), P(), P(), row, P(), P(), row, P(), P(), P(), row, P(), row, P())
    return jax.shard_map(
        per_device, mesh=mesh, in_specs=placed, out_specs=outs, check_vma=False
    )
```

```python
import jax
import jax.numpy as jnp
from jax import lax
from jax.experimental import pallas as pl
from jax.experimental.pallas import tpu as pltpu
from jax.sharding import PartitionSpec as P

HEADS = 12
FORWARD_GROUP, BACK_GROUP = 2, 2
LEADS_AT = 16
SMALL_COLUMNS = 256
LAST_SHARES = (1024, 1024, 1024)
SEQUENCE = (
    "DO", "M", "UO", "A0", "D2", "A1", "U2", "D3", "QO", "U3", "NB", "D4", "BO", "U4", "Q2",
    "DA", "Q3", "DP", "UA", "Q4", "SX", "SZ", "QA", "UP", "SO", "QP",
)
PLAIN = ("M", "A0", "A1", "NB", "BO")
SMALL_NAMES = ("gain1", "bias1", "query", "value", "out", "gain2", "bias2", "down", "up", "table")
OUTPUTS = ("block_out", "grad_patches", "gain1", "bias1", "table", "sum_qkv", "query", "value")
OUTPUTS += ("sum_out", "out", "gain2", "bias2", "sum_up", "up", "sum_down", "down")
COSTS = {"D3": 100, "DO": 30, "A1": 2}
VMEM_BYTES = 63 * 1024 * 1024


norm_epsilon = 1e-05
masked_score = -1e30

density_scale = 0.3989422804014327


def dot_nn(a, b):
    return lax.dot_general(a, b, (((1,), (0,)), ((), ())), preferred_element_type=jnp.float32)


def dot_nt(a, b):
    return lax.dot_general(a, b, (((1,), (1,)), ((), ())), preferred_element_type=jnp.float32)


def dot_tn(a, b):
    return lax.dot_general(a, b, (((0,), (0,)), ((), ())), preferred_element_type=jnp.float32)


def normalise(values):
    centre = jnp.mean(values, axis=-1, keepdims=True)
    centred = values - centre
    spread = jnp.mean(centred * centred, axis=-1, keepdims=True)
    inverse = lax.rsqrt(spread + norm_epsilon)
    return centred * inverse, inverse


def normalise_back(grad, unit, inverse):
    first = jnp.mean(grad, axis=-1, keepdims=True)
    second = jnp.mean(grad * unit, axis=-1, keepdims=True)
    return inverse * (grad - first - unit * second)


def column_sum(values):
    return jnp.sum(values, axis=0, keepdims=True)


def gelu_pair(pre):
    normal = 0.5 + 0.5 * lax.erf(pre * 0.7071067811865476)
    return pre * normal, normal + pre * (density_scale * jnp.exp(-0.5 * (pre * pre)))


def line(vector):
    return vector[...].reshape(1, -1)


def project_kernel(
    leads, patches, gain, bias, bias_query, bias_value, lead_table, w_qkv, normed, qkv
):
    window = pl.program_id(0)
    width = patches.shape[-1]
    unit, _ = normalise(patches[0].astype(jnp.float32))
    lead_row = lead_table[pl.ds(leads[window], 1), :]
    low = (unit * line(gain) + line(bias) + lead_row).astype(jnp.bfloat16)
    normed[...] = low
    queries = dot_nn(low, w_qkv[:, :width]) + line(bias_query)
    qkv[:, :width] = queries.astype(jnp.bfloat16) * 0.125
    qkv[:, width : 2 * width] = dot_nn(low, w_qkv[:, width : 2 * width]).astype(jnp.bfloat16)
    values = dot_nn(low, w_qkv[:, 2 * width :]) + line(bias_value)
    qkv[:, 2 * width :] = values.astype(jnp.bfloat16)


def each_alone(columns, place):
    zero = jnp.zeros_like(columns)
    return jnp.concatenate([jnp.where(place == i, columns, zero) for i in range(columns.shape[1] // 64)], axis=0)


def own_columns(stacked, place):
    rows = place.shape[0]
    joined = stacked[:rows]
    for i in range(1, stacked.shape[1] // 64):
        joined = jnp.where(place == i, stacked[i * rows : (i + 1) * rows], joined)
    return joined


def attend_kernel(
    lengths,
    patches,
    qkv,
    w_out,
    bias_out,
    gain,
    bias,
    attended,
    residual,
    normed2,
    turned,
    log_total,
):
    window = pl.program_id(0)
    _, rows, width = patches.shape
    keys_at = lax.broadcasted_iota(jnp.int32, (rows, 1), 0)
    blocked = jnp.where(keys_at < lengths[window], 0.0, masked_score)
    span = FORWARD_GROUP * 64
    place = lax.broadcasted_iota(jnp.int32, (rows, span), 1) // 64
    for at in range(0, width, span):
        query = each_alone(qkv[:, at : at + span], place)
        key = qkv[:, width + at : width + at + span]
        value = qkv[:, 2 * width + at : 2 * width + at + span]
        scores = dot_nt(key, query) + blocked
        top = jnp.max(scores, axis=0, keepdims=True)
        exponent = jnp.exp(scores - top)
        total = jnp.sum(exponent, axis=0, keepdims=True)
        probs = (exponent * (1.0 / total)).astype(jnp.bfloat16)
        out = own_columns(dot_tn(probs, value), place)
        attended[:, at : at + span] = out.astype(jnp.bfloat16)
        log_sum = top + jnp.log(total)
        for i in range(FORWARD_GROUP):
            head = at // 64 + i
            log_total[0, head : head + 1, :] = log_sum[:, i * rows : (i + 1) * rows]
    branch = dot_nn(attended[...], w_out[...]) + line(bias_out)
    held = patches[0].astype(jnp.float32) + branch
    residual[...] = held
    unit, _ = normalise(held)
    low = (unit * line(gain) + line(bias)).astype(jnp.bfloat16)
    normed2[...] = low
    turned[...] = low.T


def store_halves(result, here, keep, send):
    if keep.ndim == 2:
        keep[...] = result
        send[...] = jnp.zeros_like(send)
        return
    blocks, share, columns = keep.shape
    split = result.reshape(blocks, 2, share, columns)
    first, second = split[:, 0], split[:, 1]
    keep[...] = jnp.where(here == 0, first, second)
    send[...] = jnp.where(here == 0, second, first)


def mlp_kernel(
    lengths,
    scales,
    here,
    cotangent,
    normed2,
    w_up,
    bias_up,
    activated,
    slope,
    grad_down,
    keep,
    send,
):
    windows, rows, width = cotangent.shape
    step = pl.program_id(0)

    @pl.when(step == 0)
    def _():
        row = lax.broadcasted_iota(jnp.int32, (rows, 1), 0)
        for window in range(windows):
            weight = jnp.where(row < lengths[window], scales[window], 0.0)
            grad = (cotangent[window].astype(jnp.float32) * weight).astype(jnp.bfloat16)
            grad_down[window * rows : (window + 1) * rows, :] = grad

    bias = bias_up[pl.ds(pl.multiple_of(step * width, 128), width)]
    for window in range(windows):
        at = slice(window * rows, (window + 1) * rows)
        pre = dot_nn(normed2[at, :], w_up[...]) + bias.reshape(1, -1)
        out, steep = gelu_pair(pre)
        out = out.astype(jnp.bfloat16)
        activated[at, :] = out
        slope[at, :] = steep.astype(jnp.bfloat16)
    store_halves(dot_tn(activated[...], grad_down[...]), here[0], keep, send)


def mlp_back_kernel(
    here, grad_down, slope, turned, w_up, w_down, grad_bias_up, grad_normed2, keep, send
):
    step = pl.program_id(0)

    @pl.when(step == 0)
    def _():
        grad_normed2[...] = jnp.zeros_like(grad_normed2)

    grad_act = dot_nt(grad_down[...], w_down[...])
    grad_up = (grad_act * slope[...].astype(jnp.float32)).astype(jnp.bfloat16)
    grad_bias_up[0] = column_sum(grad_up.astype(jnp.float32))
    store_halves(dot_nn(turned[...], grad_up), here[0], keep, send)
    grad_normed2[...] += dot_nt(grad_up, w_up[...])


def middle_back_kernel(
    lengths,
    scales,
    here,
    cotangent,
    residual,
    grad_normed2,
    attended,
    w_out,
    gain,
    grad_residual,
    grad_attended,
    delta,
    sums,
    branch_low,
):
    window = pl.program_id(0)
    _, rows, width = cotangent.shape

    @pl.when(window == 0)
    def _():
        sums[...] = jnp.zeros_like(sums)

    row = lax.broadcasted_iota(jnp.int32, (rows, 1), 0)
    weight = jnp.where(row < lengths[window], scales[window], 0.0)
    grad_out = cotangent[0].astype(jnp.float32) * weight
    unit, inverse = normalise(residual[...])
    grad_norm = grad_normed2[...]
    held = grad_out + normalise_back(grad_norm * line(gain), unit, inverse)
    grad_residual[...] = held
    branch = held.astype(jnp.bfloat16)
    branch_low[...] = branch
    sums[0:1, :] += column_sum(grad_norm * unit)
    sums[1:2, :] += column_sum(grad_norm)
    sums[2:3, :] += column_sum(branch.astype(jnp.float32))
    sums[3:4, :] += column_sum(grad_out.astype(jnp.bfloat16).astype(jnp.float32))
    grad_att = dot_nt(branch, w_out[...]).astype(jnp.bfloat16)
    grad_attended[...] = grad_att
    product = grad_att.astype(jnp.float32) * attended[...].astype(jnp.float32)
    high = product.astype(jnp.bfloat16)
    low = (product - high.astype(jnp.float32)).astype(jnp.bfloat16)
    head = lax.broadcasted_iota(jnp.int32, (delta.shape[1], width), 0)
    column = lax.broadcasted_iota(jnp.int32, (delta.shape[1], width), 1)
    head_rows = (column // (width // HEADS) == head).astype(jnp.bfloat16)
    delta[0] = dot_nt(head_rows, high) + dot_nt(head_rows, low)


def attend_back_heads(first, lengths, refs, log_total, delta, out, columns):
    queries, keys, values, grad_attended = refs
    rows, width = queries.shape
    row = lax.broadcasted_iota(jnp.int32, (rows, 1), 0)
    blocked = jnp.where(row < lengths[pl.program_id(0)], 0.0, masked_score)
    span = BACK_GROUP * 64
    place = lax.broadcasted_iota(jnp.int32, (rows, span), 1) // 64

    def start(at):
        query = each_alone(queries[:, at : at + span], place)
        grad_group = each_alone(grad_attended[:, at : at + span], place)
        scores = dot_nt(keys[:, at : at + span], query) + blocked
        return query, grad_group, scores, dot_nt(values[:, at : at + span], grad_group)

    ahead = start(0)
    for at in range(0, width, span):
        query, grad_group, scores, grad_probs = ahead
        if at + span < width:
            ahead = start(at + span)
        heads = range(first + at // 64, first + at // 64 + BACK_GROUP)
        totals = jnp.concatenate([log_total[0, h : h + 1, :] for h in heads], axis=1)
        shift = jnp.concatenate([delta[0, h : h + 1, :] for h in heads], axis=1)
        probs = jnp.exp(scores - totals)
        grad_scores = (probs * (grad_probs - shift)).astype(jnp.bfloat16)
        grad_query = own_columns(dot_tn(grad_scores, keys[:, at : at + span]), place) * 0.125
        grad_key = dot_nn(grad_scores, query)
        grad_value = dot_nn(probs.astype(jnp.bfloat16), grad_group)
        for index, grad in enumerate((grad_query, grad_key, grad_value)):
            to = columns[index] + at
            out[:, to : to + span] = grad.astype(jnp.bfloat16)


def attend_back_first_kernel(lengths, queries, keys, values, grad_attended, log_total, delta, out):
    half = queries.shape[1]
    refs = (queries, keys, values, grad_attended)
    attend_back_heads(0, lengths, refs, log_total, delta, out, (0, half, 2 * half))


def attend_back_kernel(
    lengths,
    here,
    queries,
    keys,
    values,
    grad_attended,
    normed,
    log_total,
    delta,
    attended,
    branch,
    first,
    grad_projected,
    sums,
    keep,
    send,
    grad_w,
):
    window = pl.program_id(0)
    half = queries.shape[1]
    width = 2 * half

    @pl.when(window == 0)
    def _():
        grad_w[...] = jnp.zeros_like(grad_w)
        sums[...] = jnp.zeros_like(sums)

    refs = (queries, keys, values, grad_attended)
    columns = (half, width + half, 2 * width + half)
    attend_back_heads(HEADS // 2, lengths, refs, log_total, delta, grad_projected, columns)
    for third in range(3):
        part = first[:, third * half : (third + 1) * half]
        grad_projected[:, third * width : third * width + half] = part
    grad_w[:, : 3 * width] += dot_tn(normed[...], grad_projected[...])
    grad_w[:, 3 * width :] += dot_tn(attended[...], branch[...])
    sums[0:1, :] += column_sum(grad_projected[:, :width].astype(jnp.float32))
    sums[1:2, :] += column_sum(grad_projected[:, 2 * width :].astype(jnp.float32))

    @pl.when(window == pl.num_programs(0) - 1)
    def _():
        store_halves(grad_w[...], here[0], keep, send)


def norm_back_kernel(
    leads,
    patches,
    grad_residual,
    grad_projected,
    w_qkv,
    gain,
    middle_sums,
    bias_sums,
    bias_rows,
    grad_patches,
    small,
):
    window = pl.program_id(0)

    def put(row, value, add=False):
        for piece in range(value.shape[1] // SMALL_COLUMNS):
            at = pl.ds(row * (value.shape[1] // SMALL_COLUMNS) + piece, 1)
            part = value[:, piece * SMALL_COLUMNS : (piece + 1) * SMALL_COLUMNS]
            small[at, :] = small[at, :] + part if add else part

    @pl.when(window == 0)
    def _():
        small[...] = jnp.zeros_like(small)
        for row in range(4):
            put(row, middle_sums[row : row + 1, :])
        for row in range(2):
            put(4 + row, bias_sums[row : row + 1, :])
        for row in range(bias_rows.shape[0]):
            put(8 + row, bias_rows[row])

    grad_norm = dot_nt(grad_projected[...], w_qkv[...])
    unit, inverse = normalise(patches[0].astype(jnp.float32))
    back = normalise_back(grad_norm * line(gain), unit, inverse)
    grad_patches[0] = (grad_residual[...] + back).astype(jnp.bfloat16)
    total = column_sum(grad_norm)
    put(6, column_sum(grad_norm * unit), add=True)
    put(7, total, add=True)
    put(LEADS_AT + leads[window], total, add=True)


def block_out_kernel(activated, w_down, bias_down, residual, block_out):
    final = residual[...] + dot_nn(activated[...], w_down[...]) + line(bias_down)
    block_out[0] = final.astype(jnp.bfloat16)


Z1, Z0, X, Y = range(4)
LINKS = (("dp", 3), ("dp", 2), ("dp", 1), ("outer", 0))


def split_kernel(pairs, parts, axes, merge, gridded, riders, bits, *refs):
    outs = refs[2 * len(pairs) + (riders == "join") :]
    start = 0
    for index, (pieces, axis) in enumerate(zip(parts, axes)):
        send, keep = outs[:2] if merge else outs[2 * index : 2 * index + 2]
        if not merge:
            start = 0
        mine = bits[axis]
        for pair, first, width in pieces:
            held, come = refs[2 * pair], refs[2 * pair + 1]
            at = [slice(None)] * len(held.shape)
            if gridded:
                at[0] = 0
            at[-1] = slice(first, first + width)
            place = pairs[pair].index(axis)
            for out, side in ((send, 1 - mine), (keep, mine)):
                at[place] = side
                value = held[tuple(at)] + come[tuple(at)]
                to = (Ellipsis, slice(start, start + width))
                out[(0,) + to if gridded else to] = value
            start += width
    if riders == "join":
        rider = refs[2 * len(pairs)]
        rows, wide = outs[0].shape[0], rider.shape[1]
        for out in outs[:2]:
            for side in range(2):
                to = slice(start + side * wide, start + (side + 1) * wide)
                out[:, to] = rider[side * rows : (side + 1) * rows, :]


def add_kernel(held, come, out):
    out[...] = held[...] + come[...]


SMALL_ROWS = (6, 7, 4, 5, 2, 0, 1, 3)


def small_out_kernel(held, come, *outs):
    total = held[...] + come[...]
    columns = total.shape[1]
    vectors, bias_up, table = outs[:8], outs[8], outs[9]
    pieces = table.shape[1] // columns

    def copy(row, out, start):
        for piece in range(pieces):
            value = total[row * pieces + piece : row * pieces + piece + 1, :]
            out[pl.ds(start + piece * columns, columns)] = value.reshape(columns)

    for row, out in zip(SMALL_ROWS, vectors):
        copy(row, out, 0)
    for row in range(bias_up.shape[0] // table.shape[1]):
        copy(8 + row, bias_up, row * table.shape[1])
    for row in range(table.shape[0]):
        for piece in range(pieces):
            at = (LEADS_AT + row) * pieces + piece
            table[row : row + 1, piece * columns : (piece + 1) * columns] = total[at : at + 1, :]


def place_kernel(moves, rider, bits, own, other, *outs):
    rows = own.shape[0]
    mine = bits[Y]
    for out, to, start, width in moves:
        for value, side in ((own, mine), (other, 1 - mine)):
            outs[out][pl.ds(side * rows, rows), to : to + width] = value[:, start : start + width]
    if rider is not None:
        wide = outs[-1].shape[1]
        for side in range(2):
            at = slice(rider + side * wide, rider + (side + 1) * wide)
            outs[-1][side * rows : (side + 1) * rows, :] = own[:, at] + other[:, at]


DOWN_ORDERS, DOWN_SHARES = [(X, Y, Z0, Z1), (Y, X, Z0, Z1)], (384, 384)
UP_ORDERS, UP_SHARES = [(Z0, X, Y, Z1), (X, Z0, Y, Z1)], (1920, 1152)
LAST_ORDERS = [(X, Y, Z0, Z1), (Y, Z0, X, Z1), (Z0, X, Y, Z1)]


def swap(values, axis, bit):
    size = lax.axis_size(axis)
    return lax.ppermute(values, axis, [(i, i ^ (1 << bit)) for i in range(size)])


def bit_of(axis, bit):
    return lax.rem(lax.div(lax.axis_index(axis), 1 << bit), 2)


def dp_bits():
    return lax.axis_size("dp").bit_length() - 1


def exchange(values, dp_mask, outer_mask):
    inner = lax.axis_size("outer")
    size = lax.axis_size("dp") * inner
    flip = dp_mask * inner + outer_mask
    return lax.ppermute(values, ("dp", "outer"), [(i, i ^ flip) for i in range(size)])


def count_rounds(values):
    steps = [(1 << bit, 0) for bit in range(1, dp_bits())] + [(0, 1)]
    rounds = [[(1, 0)]] + [steps[at : at + 2] for at in range(0, len(steps), 2)]
    for group in rounds:
        flips = list(group)
        if len(group) == 2:
            flips.append((group[0][0] | group[1][0], group[0][1] | group[1][1]))
        values = values + sum(exchange(values, *flip) for flip in flips)
        yield values


def part_orders(bit_count):
    rest = list(range(3, bit_count))
    return (
        [("dp", 1), ("outer", 0), ("dp", 2)] + [("dp", b) for b in rest],
        [("outer", 0), ("dp", 2), ("dp", 1)] + [("dp", b) for b in rest],
        [("dp", 2), ("dp", 1), ("outer", 0)] + [("dp", b) for b in rest],
    )


def halve(values, dims, step):
    axis, bit = step
    place = dims.index(step)
    mine = bit_of(axis, bit)
    keep = lax.dynamic_index_in_dim(values, mine, place, keepdims=False)
    send = lax.dynamic_index_in_dim(values, 1 - mine, place, keepdims=False)
    left = dims[:place] + dims[place + 1 :]
    return keep + swap(send, axis, bit), left


def scatter_sum(matrix):
    bit_count = dp_bits()
    rows, columns = matrix.shape
    share = rows // lax.axis_size("dp")
    dims = [("dp", b) for b in range(bit_count - 1, -1, -1)] + [("outer", 0)]
    values = matrix.reshape((2,) * bit_count + (2, share // 2, columns))
    values, dims = halve(values, dims, ("dp", 0))
    third = columns // 3
    pieces = []
    for index, order in enumerate(part_orders(bit_count)):
        part = lax.slice_in_dim(values, index * third, (index + 1) * third, axis=values.ndim - 1)
        left = dims
        for step in order:
            part, left = halve(part, left, step)
        pieces.append(part)
    mine = jnp.concatenate(pieces, axis=1)
    other = swap(mine, "outer", 0)
    first = lax.axis_index("outer") == 0
    return jnp.concatenate([jnp.where(first, mine, other), jnp.where(first, other, mine)], axis=0)


def per_device(
    patches,
    lengths,
    leads,
    counts,
    cotangent,
    norm1_gain,
    norm1_bias,
    lead_table,
    w_qkv,
    bias_query,
    bias_value,
    w_out,
    bias_out,
    norm2_gain,
    norm2_bias,
    w_up,
    bias_up,
    w_down,
    bias_down,
):
    slots, rows, width = patches.shape
    total = slots * rows
    hidden = w_up.shape[1]
    lead_count = lead_table.shape[0]
    steps = hidden // width
    f32, bf16 = jnp.float32, jnp.bfloat16
    parts = lax.axis_size("dp")
    share = width // parts
    fast = parts == 16 and share % 16 == 0 and slots == 4

    smem = pl.BlockSpec(memory_space=pltpu.SMEM)
    params = pltpu.CompilerParams(vmem_limit_bytes=VMEM_BYTES)

    def whole(*shape):
        return pl.BlockSpec(shape, lambda *i: (0,) * len(shape))

    def by_window(columns, at=0):
        return pl.BlockSpec((rows, columns), lambda i: (i, at))

    current = [""]

    def call(kernel, grid, inputs, outs, scratch=(), after=(), carry=()):
        count, extra, carried = len(inputs), len(after) + len(carry), len(carry)
        made = count + extra + len(outs)

        def body(*refs):
            kernel(*refs[:count], *refs[count + extra : made], *refs[made + carried :])

        anywhere = pl.BlockSpec(memory_space=pl.ANY)
        return pl.pallas_call(
            body,
            grid=grid,
            in_specs=[spec for spec, _ in inputs] + [anywhere] * extra,
            out_specs=[spec for spec, _, _ in outs] + [anywhere] * carried,
            out_shape=[jax.ShapeDtypeStruct(shape, dtype) for _, shape, dtype in outs]
            + [jax.ShapeDtypeStruct(value.shape, value.dtype) for value in carry],
            input_output_aliases={
                count + len(after) + i: len(outs) + i for i in range(carried)
            },
            scratch_shapes=scratch,
            compiler_params=params,
            cost_estimate=pl.CostEstimate(
                flops=int(COSTS.get(current[0], 0) * 1.15e9), bytes_accessed=0, transcendentals=0
            ),
        )(*[value for _, value in inputs], *after, *carry)

    live = jnp.arange(slots, dtype=jnp.int32) < counts[0]
    onehot = (leads[:, None] == jnp.arange(lead_count, dtype=jnp.int32)[None, :]).astype(f32)
    rounds = count_rounds(jnp.sum(onehot * live[:, None].astype(f32), axis=0))
    counted = next(rounds)

    dp_at, outer_at = lax.axis_index("dp"), lax.axis_index("outer")
    here = lax.rem(dp_at, 2).reshape(1)
    bits = jnp.stack([bit_of("dp", 3), bit_of("dp", 2), bit_of("dp", 1), outer_at])
    def flat(vector):
        return whole(*vector.shape), vector

    by_slot = pl.BlockSpec((1, rows, width), lambda i: (i, 0, 0))
    by_head = pl.BlockSpec((1, 16, rows), lambda i: (i, 0, 0))

    def halves(blocks, columns, grid_axis=None):
        if not fast:
            spec = pl.BlockSpec((width, columns), lambda i: (0, 0))
            return [(spec, (width, columns), f32), (whole(8, 128), (8, 128), f32)]
        shape = (parts // 2, share, columns)
        return [(whole(*shape), shape, f32)] * 2

    normed, qkv = call(
        project_kernel,
        (slots,),
        [
            (smem, leads),
            (by_slot, patches),
            flat(norm1_gain),
            flat(norm1_bias),
            flat(bias_query),
            flat(bias_value),
            (whole(*lead_table.shape), lead_table),
            (whole(*w_qkv.shape), w_qkv),
        ],
        [
            (by_window(width), (total, width), bf16),
            (by_window(3 * width), (total, 3 * width), bf16),
        ],
        after=[counted],
    )
    counted = next(rounds)
    attended, residual, normed2, turned, log_total = call(
        attend_kernel,
        (slots,),
        [
            (smem, lengths),
            (by_slot, patches),
            (by_window(3 * width), qkv),
            (whole(*w_out.shape), w_out),
            flat(bias_out),
            flat(norm2_gain),
            flat(norm2_bias),
        ],
        [
            (by_window(width), (total, width), bf16),
            (by_window(width), (total, width), f32),
            (by_window(width), (total, width), bf16),
            (pl.BlockSpec((width, rows), lambda i: (0, i)), (width, total), bf16),
            (by_head, (slots, 16, rows), f32),
        ],
        after=[counted],
    )
    for counted in rounds:
        pass
    window_total = jnp.sum(onehot * counted[None, :], axis=1)
    scales = jnp.where(live, 1.0 / jnp.maximum(window_total, 1.0), 0.0)

    by_lanes = pl.BlockSpec((total, width), lambda i: (0, i))
    up_spec = pl.BlockSpec((width, width), lambda i: (0, i))
    if fast:
        pair_share = hidden // parts
        pair_shape = (parts // 2, pair_share, width)
        pair_spec = pl.BlockSpec((parts // 2 // steps, pair_share, width), lambda i: (i, 0, 0))
        down_halves = [(pair_spec, pair_shape, f32)] * 2
    else:
        down_spec = pl.BlockSpec((width, width), lambda i: (i, 0))
        down_halves = [(down_spec, (hidden, width), f32), (whole(8, 128), (8, 128), f32)]
    activated, slope, grad_down, keep_down, send_down = call(
        mlp_kernel,
        (steps,),
        [
            (smem, lengths),
            (smem, scales),
            (smem, here),
            (whole(*cotangent.shape), cotangent),
            (whole(total, width), normed2),
            (up_spec, w_up),
            flat(bias_up),
        ],
        [
            (by_lanes, (total, hidden), bf16),
            (by_lanes, (total, hidden), bf16),
            (whole(total, width), (total, width), bf16),
        ]
        + down_halves,
    )
    if fast:
        shape = (parts // 2, share, hidden)
        up_halves = [(pl.BlockSpec((parts // 2, share, width), lambda i: (0, 0, i)), shape, f32)] * 2
    else:
        up_halves = [(up_spec, (width, hidden), f32), (whole(8, 128), (8, 128), f32)]
    grad_bias_up, grad_normed2, keep_up, send_up = call(
        mlp_back_kernel,
        (steps,),
        [
            (smem, here),
            (whole(total, width), grad_down),
            (by_lanes, slope),
            (whole(width, total), turned),
            (up_spec, w_up),
            (pl.BlockSpec((width, width), lambda i: (i, 0)), w_down),
        ],
        [
            (pl.BlockSpec((1, 1, width), lambda i: (i, 0, 0)), (steps, 1, width), f32),
            (whole(total, width), (total, width), f32),
        ]
        + up_halves,
    )

    def core_swap(send):
        return swap(send, "dp", 0) if fast else send

    def split_round(pairs, dims, parts, axes, done, rider=None):
        riders = "join" if rider is not None else None
        merge = len(set(axes)) == 1 and len({tuple(dims[p[0][0]]) for p in parts}) == 1
        gridded = all(d[0] == Z1 and len(d) > 1 for d in dims) and Z1 not in axes and not riders
        rows_here = pairs[0][0].shape[-2]
        widths = [sum(width for _, _, width in part) for part in parts]
        left = [[d for d in dims[part[0][0]] if d != axis] for part, axis in zip(parts, axes)]
        if merge:
            widths, left = [sum(widths)], left[:1]
            if riders == "join":
                widths = [widths[0] + 2 * rider.shape[-1]]
        shapes = [(2,) * len(d) + (rows_here, width) for d, width in zip(left, widths)]

        def spec(shape):
            if not gridded:
                return whole(*shape)
            return pl.BlockSpec((1,) + shape[1:], lambda i: (i,) + (0,) * (len(shape) - 1))

        inputs = [(smem, bits)] + [(spec(v.shape), v) for pair in pairs for v in pair]
        if riders == "join":
            inputs.append((spec(rider.shape), rider))
        outs = [(spec(shape), shape, f32) for shape in shapes for _ in range(2)]

        def kernel(*refs):
            split_kernel(dims, parts, axes, merge, gridded, riders, *refs)

        def finish(values):
            done([(values[2 * i], values[2 * i + 1]) for i in range(len(shapes))], left)
            return list(values)

        return kernel, (2,) if gridded else (), inputs, outs, [], finish

    class Chunk:
        def __init__(self, sources, orders, shares):
            self.sources, self.orders, self.step_count = sources, orders, 0
            self.columns = [[] for _ in orders]
            for i, cuts in enumerate(shares):
                start = 0
                for pieces, width in zip(self.columns, cuts):
                    pieces.append((i, start, width))
                    start += width

        def open(self):
            shaped = lambda v: v.reshape((2, 2, 2, 2, -1, v.shape[-1]))
            pairs = [(shaped(keep), shaped(come)) for keep, come in self.sources]
            axes = [order[0] for order in self.orders]
            dims = [[Z1, Z0, X, Y]] * len(pairs)
            return split_round(pairs, dims, self.columns, axes, self.put)

        def put(self, states, dims):
            self.states, self.dims = states, dims
            self.axes = [order[self.step_count] for order in self.orders][: len(states)]
            self.step_count += 1

        def pairs(self):
            return [
                (keep, swap(send, *LINKS[axis]))
                for (send, keep), axis in zip(self.states, self.axes)
            ]

        def step(self, rider=None):
            pairs = self.pairs()
            axes = [order[self.step_count] for order in self.orders][: len(pairs)]
            parts = [[(i, 0, keep.shape[-1])] for i, (keep, _) in enumerate(pairs)]
            return split_round(pairs, self.dims, parts, axes, self.put, rider)

        def add(self):
            ((keep, come),) = self.pairs()
            spec = whole(*keep.shape)

            def finish(values):
                (self.own,) = values
                return values

            inputs = [(spec, keep), (spec, come)]
            return add_kernel, (), inputs, [(spec, keep.shape, f32)], [], finish

        def place(self, outputs, finish, rider=False):
            own = self.own
            other = swap(own, *LINKS[Y])
            moves, start = [], 0
            for pieces in self.columns:
                for source, first, wide in pieces:
                    for out, (origin, low, size) in enumerate(outputs):
                        begin, end = max(first, low), min(first + wide, low + size)
                        if origin == source and begin < end:
                            moves.append((out, begin - low, start + begin - first, end - begin))
                    start += wide
            shapes = [(2 * own.shape[0], size) for _, _, size in outputs]
            if rider:
                shapes.append((2 * own.shape[0], (own.shape[1] - start) // 2))

            def kernel(*refs):
                place_kernel(moves, start if rider else None, *refs)

            inputs = [(smem, bits), (whole(*own.shape), own), (whole(*other.shape), other)]
            outs = [(whole(*shape), shape, f32) for shape in shapes]
            return kernel, (), inputs, outs, [], finish

    come_down = core_swap(send_down)
    come_up = core_swap(send_up)
    made = {}

    def keep_results(*names):
        def finish(values):
            made.update(zip(names, values))
            return list(values[:1])

        return finish

    def middle():
        return (
            middle_back_kernel,
            (slots,),
            [
                (smem, lengths),
                (smem, scales),
                (smem, here),
                (by_slot, cotangent),
                (by_window(width), residual),
                (by_window(width), grad_normed2),
                (by_window(width), attended),
                (whole(*w_out.shape), w_out),
                flat(norm2_gain),
            ],
            [
                (by_window(width), (total, width), f32),
                (by_window(width), (total, width), bf16),
                (by_head, (slots, 16, rows), f32),
                (whole(8, width), (8, width), f32),
                (by_window(width), (total, width), bf16),
            ],
            [],
            keep_results("grad_residual", "grad_attended", "delta", "sums", "branch"),
        )

    half = width // 2

    def attention_first():
        return (
            attend_back_first_kernel,
            (slots,),
            [
                (smem, lengths),
                (by_window(half, 0), qkv),
                (by_window(half, 2), qkv),
                (by_window(half, 4), qkv),
                (by_window(half, 0), made["grad_attended"]),
                (by_head, log_total),
                (by_head, made["delta"]),
            ],
            [(by_window(3 * half), (total, 3 * half), bf16)],
            [],
            keep_results("projected_first"),
        )

    def attention():
        return (
            attend_back_kernel,
            (slots,),
            [
                (smem, lengths),
                (smem, here),
                (by_window(half, 1), qkv),
                (by_window(half, 3), qkv),
                (by_window(half, 5), qkv),
                (by_window(half, 1), made["grad_attended"]),
                (by_window(width), normed),
                (by_head, log_total),
                (by_head, made["delta"]),
                (by_window(width), attended),
                (by_window(width), made["branch"]),
                (by_window(3 * half), made["projected_first"]),
            ],
            [
                (by_window(3 * width), (total, 3 * width), bf16),
                (whole(8, width), (8, width), f32),
            ]
            + halves(parts // 2, 4 * width),
            [pltpu.VMEM((width, 4 * width), f32)],
            keep_results("grad_projected", "bias_sums", "keep_last", "send_last"),
        )

    def first_norm():
        small_rows = 64 * width // SMALL_COLUMNS
        return (
            norm_back_kernel,
            (slots,),
            [
                (smem, leads),
                (by_slot, patches),
                (by_window(width), made["grad_residual"]),
                (by_window(3 * width), made["grad_projected"]),
                (whole(*w_qkv.shape), w_qkv),
                flat(norm1_gain),
                (whole(*made["sums"].shape), made["sums"]),
                (whole(*made["bias_sums"].shape), made["bias_sums"]),
                (whole(*grad_bias_up.shape), grad_bias_up),
            ],
            [
                (by_slot, patches.shape, bf16),
                (whole(small_rows, SMALL_COLUMNS), (small_rows, SMALL_COLUMNS), f32),
            ],
            [],
            keep_results("grad_patches", "small"),
        )

    def output():
        return (
            block_out_kernel,
            (slots,),
            [
                (by_window(hidden), activated),
                (whole(*w_down.shape), w_down),
                flat(bias_down),
                (by_window(width), residual),
            ],
            [(by_slot, patches.shape, bf16)],
            [],
            keep_results("block_out"),
        )

    def add_small(bit):
        small = made["small"]
        spec = whole(*small.shape)
        inputs = [(spec, small), (spec, swap(small, "dp", bit))]
        return add_kernel, (), inputs, [(spec, small.shape, f32)], [], keep_results("small")

    def small_outs():
        small = made["small"]
        spec = whole(*small.shape)
        shapes = [(width,)] * 8 + [bias_up.shape, lead_table.shape]
        outs = [(whole(*shape), shape, f32) for shape in shapes]
        inputs = [(spec, small), (spec, swap(small, "dp", 0))]
        return small_out_kernel, (), inputs, outs, [], keep_results(*SMALL_NAMES)

    def run(works, after):
        counts = [[len(work[part]) for work in works] for part in (2, 3, 4)]

        def kernel(*refs):
            at = 0
            groups = [[] for _ in works]
            for part in counts:
                for group, count in zip(groups, part):
                    group.extend(refs[at : at + count])
                    at += count
            for work, group in zip(works, groups):
                work[0](*group)

        joined = [[item for work in works for item in work[part]] for part in (2, 3, 4)]
        values = call(kernel, works[0][1], *joined, after=after)
        tokens, at = [], 0
        for work, count in zip(works, counts[1]):
            tokens += work[5](values[at : at + count])
            at += count
        return tokens

    def build(event):
        name, step = event[0], event[1:]
        if event in PLAIN:
            works = (middle, attention_first, attention, first_norm, output)
            return works[PLAIN.index(event)]()
        if name == "S":
            return small_outs() if step == "O" else add_small({"X": 1, "Z": 2}[step])
        if step == "O":
            keep, send, orders, shares = {
                "D": (keep_down, send_down, DOWN_ORDERS, DOWN_SHARES),
                "U": (keep_up, send_up, UP_ORDERS, UP_SHARES),
                "Q": (made.get("keep_last"), made.get("send_last"), LAST_ORDERS, LAST_SHARES),
            }[name]
            chunks[name] = Chunk([(keep, core_swap(send))], orders, [shares])
            return chunks[name].open()
        chunk = chunks[name]
        if step == "A":
            return chunk.add()
        if event == "DP":
            return chunk.place([(0, 0, width)], keep_results("sum_down", "small"), rider=True)
        if event == "UP":
            return chunk.place([(0, 0, hidden)], keep_results("sum_up"))
        if event == "QP":
            outputs = [(0, 0, 3 * width), (0, 3 * width, width)]
            return chunk.place(outputs, keep_results("sum_qkv", "sum_out"))
        return chunk.step(made["small"] if event == "D4" else None)

    chunks = {}
    tokens = [grad_normed2]
    for group in SEQUENCE if fast else PLAIN:
        current[0] = group
        tokens = run([build(event) for event in group.split("+")], tokens)
    if not fast:
        for bit in range(1, dp_bits()):
            made["small"] = made["small"] + swap(made["small"], "dp", bit)
        made["small"] = made["small"] + swap(made["small"], "outer", 0)
        run([small_outs()], ())
        made["sum_down"] = scatter_sum(keep_down)
        made["sum_up"] = scatter_sum(keep_up)
        joined = scatter_sum(made["keep_last"])
        made["sum_qkv"], made["sum_out"] = joined[:, : 3 * width], joined[:, 3 * width :]
    return tuple(made[name] for name in OUTPUTS)


def solution(mesh):
    split = P(("dp", "outer"))
    placed = (split,) * 5 + (P(),) * 14
    row = P("dp", None)
    outs = (split, split, P(), P(), P(), row, P(), P(), row, P(), P(), P(), row, P(), row, P())
    return jax.shard_map(
        per_device, mesh=mesh, in_specs=placed, out_specs=outs, check_vma=False
    )
```

```python
import jax
import jax.numpy as jnp
from jax import lax
from jax.experimental import pallas as pl
from jax.experimental.pallas import tpu as pltpu
from jax.sharding import PartitionSpec as P

HEADS = 12
FORWARD_GROUP, BACK_GROUP = 2, 2
LEADS_AT = 16
SMALL_COLUMNS = 256
LAST_SHARES = (1024, 1024, 1024)
SEQUENCE = (
    "DO", "M", "UO", "A0", "D2", "A1", "U2", "D3", "QO", "U3", "NB", "D4", "BO", "U4", "Q2",
    "DA", "Q3", "DP", "UA", "Q4", "SX", "SZ", "QA", "UP", "SO", "QP",
)
PLAIN = ("M", "A0", "A1", "NB", "BO")
SMALL_NAMES = ("gain1", "bias1", "query", "value", "out", "gain2", "bias2", "down", "up", "table")
OUTPUTS = ("block_out", "grad_patches", "gain1", "bias1", "table", "sum_qkv", "query", "value")
OUTPUTS += ("sum_out", "out", "gain2", "bias2", "sum_up", "up", "sum_down", "down")
COSTS = {"D3": 100, "DO": 30, "A1": 2}
VMEM_BYTES = 255 * 256 * 1024


norm_epsilon = 1e-05
masked_score = -1e30

density_scale = 0.3989422804014327


def dot_nn(a, b):
    return lax.dot_general(a, b, (((1,), (0,)), ((), ())), preferred_element_type=jnp.float32)


def dot_nt(a, b):
    return lax.dot_general(a, b, (((1,), (1,)), ((), ())), preferred_element_type=jnp.float32)


def dot_tn(a, b):
    return lax.dot_general(a, b, (((0,), (0,)), ((), ())), preferred_element_type=jnp.float32)


def normalise(values):
    centre = jnp.mean(values, axis=-1, keepdims=True)
    centred = values - centre
    spread = jnp.mean(centred * centred, axis=-1, keepdims=True)
    inverse = lax.rsqrt(spread + norm_epsilon)
    return centred * inverse, inverse


def normalise_back(grad, unit, inverse):
    first = jnp.mean(grad, axis=-1, keepdims=True)
    second = jnp.mean(grad * unit, axis=-1, keepdims=True)
    return inverse * (grad - first - unit * second)


def column_sum(values):
    return jnp.sum(values, axis=0, keepdims=True)


def gelu_pair(pre):
    normal = 0.5 + 0.5 * lax.erf(pre * 0.7071067811865476)
    return pre * normal, normal + pre * (density_scale * jnp.exp(-0.5 * (pre * pre)))


def line(vector):
    return vector[...].reshape(1, -1)


def project_kernel(
    leads, patches, gain, bias, bias_query, bias_value, lead_table, w_qkv, normed, qkv
):
    window = pl.program_id(0)
    width = patches.shape[-1]
    unit, _ = normalise(patches[0].astype(jnp.float32))
    lead_row = lead_table[pl.ds(leads[window], 1), :]
    low = (unit * line(gain) + line(bias) + lead_row).astype(jnp.bfloat16)
    normed[...] = low
    queries = dot_nn(low, w_qkv[:, :width]) + line(bias_query)
    qkv[:, :width] = queries.astype(jnp.bfloat16) * 0.125
    qkv[:, width : 2 * width] = dot_nn(low, w_qkv[:, width : 2 * width]).astype(jnp.bfloat16)
    values = dot_nn(low, w_qkv[:, 2 * width :]) + line(bias_value)
    qkv[:, 2 * width :] = values.astype(jnp.bfloat16)


def each_alone(columns, place):
    zero = jnp.zeros_like(columns)
    return jnp.concatenate([jnp.where(place == i, columns, zero) for i in range(columns.shape[1] // 64)], axis=0)


def own_columns(stacked, place):
    rows = place.shape[0]
    joined = stacked[:rows]
    for i in range(1, stacked.shape[1] // 64):
        joined = jnp.where(place == i, stacked[i * rows : (i + 1) * rows], joined)
    return joined


def attend_kernel(
    lengths,
    patches,
    qkv,
    w_out,
    bias_out,
    gain,
    bias,
    attended,
    residual,
    normed2,
    turned,
    log_total,
):
    window = pl.program_id(0)
    _, rows, width = patches.shape
    keys_at = lax.broadcasted_iota(jnp.int32, (rows, 1), 0)
    blocked = jnp.where(keys_at < lengths[window], 0.0, masked_score)
    span = FORWARD_GROUP * 64
    place = lax.broadcasted_iota(jnp.int32, (rows, span), 1) // 64
    for at in range(0, width, span):
        query = each_alone(qkv[:, at : at + span], place)
        key = qkv[:, width + at : width + at + span]
        value = qkv[:, 2 * width + at : 2 * width + at + span]
        scores = dot_nt(key, query) + blocked
        top = jnp.max(scores, axis=0, keepdims=True)
        exponent = jnp.exp(scores - top)
        total = jnp.sum(exponent, axis=0, keepdims=True)
        probs = (exponent * (1.0 / total)).astype(jnp.bfloat16)
        out = own_columns(dot_tn(probs, value), place)
        attended[:, at : at + span] = out.astype(jnp.bfloat16)
        log_sum = top + jnp.log(total)
        for i in range(FORWARD_GROUP):
            head = at // 64 + i
            log_total[0, head : head + 1, :] = log_sum[:, i * rows : (i + 1) * rows]
    branch = dot_nn(attended[...], w_out[...]) + line(bias_out)
    held = patches[0].astype(jnp.float32) + branch
    residual[...] = held
    unit, _ = normalise(held)
    low = (unit * line(gain) + line(bias)).astype(jnp.bfloat16)
    normed2[...] = low
    turned[...] = low.T


def store_halves(result, here, keep, send):
    if keep.ndim == 2:
        keep[...] = result
        send[...] = jnp.zeros_like(send)
        return
    blocks, share, columns = keep.shape
    split = result.reshape(blocks, 2, share, columns)
    first, second = split[:, 0], split[:, 1]
    keep[...] = jnp.where(here == 0, first, second)
    send[...] = jnp.where(here == 0, second, first)


def mlp_kernel(
    lengths,
    scales,
    here,
    cotangent,
    normed2,
    w_up,
    bias_up,
    activated,
    slope,
    grad_down,
    keep,
    send,
):
    windows, rows, width = cotangent.shape
    step = pl.program_id(0)

    @pl.when(step == 0)
    def _():
        row = lax.broadcasted_iota(jnp.int32, (rows, 1), 0)
        for window in range(windows):
            weight = jnp.where(row < lengths[window], scales[window], 0.0)
            grad = (cotangent[window].astype(jnp.float32) * weight).astype(jnp.bfloat16)
            grad_down[window * rows : (window + 1) * rows, :] = grad

    bias = bias_up[pl.ds(pl.multiple_of(step * width, 128), width)]
    for window in range(windows):
        at = slice(window * rows, (window + 1) * rows)
        pre = dot_nn(normed2[at, :], w_up[...]) + bias.reshape(1, -1)
        out, steep = gelu_pair(pre)
        out = out.astype(jnp.bfloat16)
        activated[at, :] = out
        slope[at, :] = steep.astype(jnp.bfloat16)
    store_halves(dot_tn(activated[...], grad_down[...]), here[CORE], keep, send)


def mlp_back_kernel(
    here, grad_down, slope, turned, w_up, w_down, grad_bias_up, grad_normed2, keep, send
):
    step = pl.program_id(0)

    @pl.when(step == 0)
    def _():
        grad_normed2[...] = jnp.zeros_like(grad_normed2)

    grad_act = dot_nt(grad_down[...], w_down[...])
    grad_up = (grad_act * slope[...].astype(jnp.float32)).astype(jnp.bfloat16)
    grad_bias_up[0] = column_sum(grad_up.astype(jnp.float32))
    store_halves(dot_nn(turned[...], grad_up), here[CORE], keep, send)
    grad_normed2[...] += dot_nt(grad_up, w_up[...])


def middle_back_kernel(
    lengths,
    scales,
    here,
    cotangent,
    residual,
    grad_normed2,
    attended,
    w_out,
    gain,
    grad_residual,
    grad_attended,
    delta,
    sums,
    branch_low,
):
    window = pl.program_id(0)
    _, rows, width = cotangent.shape

    @pl.when(window == 0)
    def _():
        sums[...] = jnp.zeros_like(sums)

    row = lax.broadcasted_iota(jnp.int32, (rows, 1), 0)
    weight = jnp.where(row < lengths[window], scales[window], 0.0)
    grad_out = cotangent[0].astype(jnp.float32) * weight
    unit, inverse = normalise(residual[...])
    grad_norm = grad_normed2[...]
    held = grad_out + normalise_back(grad_norm * line(gain), unit, inverse)
    grad_residual[...] = held
    branch = held.astype(jnp.bfloat16)
    branch_low[...] = branch
    sums[0:1, :] += column_sum(grad_norm * unit)
    sums[1:2, :] += column_sum(grad_norm)
    sums[2:3, :] += column_sum(branch.astype(jnp.float32))
    sums[3:4, :] += column_sum(grad_out.astype(jnp.bfloat16).astype(jnp.float32))
    grad_att = dot_nt(branch, w_out[...]).astype(jnp.bfloat16)
    grad_attended[...] = grad_att
    product = grad_att.astype(jnp.float32) * attended[...].astype(jnp.float32)
    high = product.astype(jnp.bfloat16)
    low = (product - high.astype(jnp.float32)).astype(jnp.bfloat16)
    head = lax.broadcasted_iota(jnp.int32, (delta.shape[1], width), 0)
    column = lax.broadcasted_iota(jnp.int32, (delta.shape[1], width), 1)
    head_rows = (column // (width // HEADS) == head).astype(jnp.bfloat16)
    delta[0] = dot_nt(head_rows, high) + dot_nt(head_rows, low)


def attend_back_heads(first, lengths, refs, log_total, delta, out, columns):
    queries, keys, values, grad_attended = refs
    rows, width = queries.shape
    row = lax.broadcasted_iota(jnp.int32, (rows, 1), 0)
    blocked = jnp.where(row < lengths[pl.program_id(0)], 0.0, masked_score)
    span = BACK_GROUP * 64
    place = lax.broadcasted_iota(jnp.int32, (rows, span), 1) // 64

    def start(at):
        query = each_alone(queries[:, at : at + span], place)
        grad_group = each_alone(grad_attended[:, at : at + span], place)
        scores = dot_nt(keys[:, at : at + span], query) + blocked
        return query, grad_group, scores, dot_nt(values[:, at : at + span], grad_group)

    ahead = start(0)
    for at in range(0, width, span):
        query, grad_group, scores, grad_probs = ahead
        if at + span < width:
            ahead = start(at + span)
        heads = range(first + at // 64, first + at // 64 + BACK_GROUP)
        totals = jnp.concatenate([log_total[0, h : h + 1, :] for h in heads], axis=1)
        shift = jnp.concatenate([delta[0, h : h + 1, :] for h in heads], axis=1)
        probs = jnp.exp(scores - totals)
        grad_scores = (probs * (grad_probs - shift)).astype(jnp.bfloat16)
        grad_query = own_columns(dot_tn(grad_scores, keys[:, at : at + span]), place) * 0.125
        grad_key = dot_nn(grad_scores, query)
        grad_value = dot_nn(probs.astype(jnp.bfloat16), grad_group)
        for index, grad in enumerate((grad_query, grad_key, grad_value)):
            to = columns[index] + at
            out[:, to : to + span] = grad.astype(jnp.bfloat16)


def attend_back_first_kernel(lengths, queries, keys, values, grad_attended, log_total, delta, out):
    half = queries.shape[1]
    refs = (queries, keys, values, grad_attended)
    attend_back_heads(0, lengths, refs, log_total, delta, out, (0, half, 2 * half))


def attend_back_kernel(
    lengths,
    here,
    queries,
    keys,
    values,
    grad_attended,
    normed,
    log_total,
    delta,
    attended,
    branch,
    first,
    grad_projected,
    sums,
    keep,
    send,
    grad_w,
):
    window = pl.program_id(0)
    half = queries.shape[1]
    width = 2 * half

    @pl.when(window == 0)
    def _():
        grad_w[...] = jnp.zeros_like(grad_w)
        sums[...] = jnp.zeros_like(sums)

    refs = (queries, keys, values, grad_attended)
    columns = (half, width + half, 2 * width + half)
    attend_back_heads(HEADS // 2, lengths, refs, log_total, delta, grad_projected, columns)
    for third in range(3):
        part = first[:, third * half : (third + 1) * half]
        grad_projected[:, third * width : third * width + half] = part
    grad_w[:, : 3 * width] += dot_tn(normed[...], grad_projected[...])
    grad_w[:, 3 * width :] += dot_tn(attended[...], branch[...])
    sums[0:1, :] += column_sum(grad_projected[:, :width].astype(jnp.float32))
    sums[1:2, :] += column_sum(grad_projected[:, 2 * width :].astype(jnp.float32))

    @pl.when(window == pl.num_programs(0) - 1)
    def _():
        store_halves(grad_w[...], here[CORE], keep, send)


def norm_back_kernel(
    leads,
    patches,
    grad_residual,
    grad_projected,
    w_qkv,
    gain,
    middle_sums,
    bias_sums,
    bias_rows,
    grad_patches,
    small,
):
    window = pl.program_id(0)

    def put(row, value, add=False):
        for piece in range(value.shape[1] // SMALL_COLUMNS):
            at = pl.ds(row * (value.shape[1] // SMALL_COLUMNS) + piece, 1)
            part = value[:, piece * SMALL_COLUMNS : (piece + 1) * SMALL_COLUMNS]
            small[at, :] = small[at, :] + part if add else part

    @pl.when(window == 0)
    def _():
        small[...] = jnp.zeros_like(small)
        for row in range(4):
            put(row, middle_sums[row : row + 1, :])
        for row in range(2):
            put(4 + row, bias_sums[row : row + 1, :])
        for row in range(bias_rows.shape[0]):
            put(8 + row, bias_rows[row])

    grad_norm = dot_nt(grad_projected[...], w_qkv[...])
    unit, inverse = normalise(patches[0].astype(jnp.float32))
    back = normalise_back(grad_norm * line(gain), unit, inverse)
    grad_patches[0] = (grad_residual[...] + back).astype(jnp.bfloat16)
    total = column_sum(grad_norm)
    put(6, column_sum(grad_norm * unit), add=True)
    put(7, total, add=True)
    put(LEADS_AT + leads[window], total, add=True)


def block_out_kernel(activated, w_down, bias_down, residual, block_out):
    final = residual[...] + dot_nn(activated[...], w_down[...]) + line(bias_down)
    block_out[0] = final.astype(jnp.bfloat16)


Z1, Z0, X, Y, CORE = range(5)
LINKS = (("dp", 3), ("dp", 2), ("dp", 1), ("outer", 0))


def split_kernel(pairs, parts, axes, merge, gridded, riders, bits, *refs):
    outs = refs[2 * len(pairs) + (riders == "join") :]
    start = 0
    for index, (pieces, axis) in enumerate(zip(parts, axes)):
        send, keep = outs[:2] if merge else outs[2 * index : 2 * index + 2]
        if not merge:
            start = 0
        mine = bits[axis]
        for pair, first, width in pieces:
            held, come = refs[2 * pair], refs[2 * pair + 1]
            at = [slice(None)] * len(held.shape)
            if gridded:
                at[0] = 0
            at[-1] = slice(first, first + width)
            place = pairs[pair].index(axis)
            for out, side in ((send, 1 - mine), (keep, mine)):
                at[place] = side
                value = held[tuple(at)] + come[tuple(at)]
                to = (Ellipsis, slice(start, start + width))
                out[(0,) + to if gridded else to] = value
            start += width
    if riders == "join":
        rider = refs[2 * len(pairs)]
        rows, wide = outs[0].shape[0], rider.shape[1]
        for out in outs[:2]:
            for side in range(2):
                to = slice(start + side * wide, start + (side + 1) * wide)
                out[:, to] = rider[side * rows : (side + 1) * rows, :]


def add_kernel(held, come, out):
    out[...] = held[...] + come[...]


SMALL_ROWS = (6, 7, 4, 5, 2, 0, 1, 3)


def small_out_kernel(held, come, *outs):
    total = held[...] + come[...]
    columns = total.shape[1]
    vectors, bias_up, table = outs[:8], outs[8], outs[9]
    pieces = table.shape[1] // columns

    def copy(row, out, start):
        for piece in range(pieces):
            value = total[row * pieces + piece : row * pieces + piece + 1, :]
            out[pl.ds(start + piece * columns, columns)] = value.reshape(columns)

    for row, out in zip(SMALL_ROWS, vectors):
        copy(row, out, 0)
    for row in range(bias_up.shape[0] // table.shape[1]):
        copy(8 + row, bias_up, row * table.shape[1])
    for row in range(table.shape[0]):
        for piece in range(pieces):
            at = (LEADS_AT + row) * pieces + piece
            table[row : row + 1, piece * columns : (piece + 1) * columns] = total[at : at + 1, :]


def place_kernel(moves, rider, bits, own, other, *outs):
    rows = own.shape[0]
    mine = bits[Y]
    for out, to, start, width in moves:
        for value, side in ((own, mine), (other, 1 - mine)):
            outs[out][pl.ds(side * rows, rows), to : to + width] = value[:, start : start + width]
    if rider is not None:
        wide = outs[-1].shape[1]
        for side in range(2):
            at = slice(rider + side * wide, rider + (side + 1) * wide)
            outs[-1][side * rows : (side + 1) * rows, :] = own[:, at] + other[:, at]


DOWN_ORDERS, DOWN_SHARES = [(X, Y, Z0, Z1), (Y, X, Z0, Z1)], (384, 384)
UP_ORDERS, UP_SHARES = [(Z0, X, Y, Z1), (X, Z0, Y, Z1)], (1920, 1152)
LAST_ORDERS = [(X, Y, Z0, Z1), (Y, Z0, X, Z1), (Z0, X, Y, Z1)]


def swap(values, axis, bit):
    size = lax.axis_size(axis)
    return lax.ppermute(values, axis, [(i, i ^ (1 << bit)) for i in range(size)])


def bit_of(axis, bit):
    return lax.rem(lax.div(lax.axis_index(axis), 1 << bit), 2)


def dp_bits():
    return lax.axis_size("dp").bit_length() - 1


def exchange(values, dp_mask, outer_mask):
    inner = lax.axis_size("outer")
    size = lax.axis_size("dp") * inner
    flip = dp_mask * inner + outer_mask
    return lax.ppermute(values, ("dp", "outer"), [(i, i ^ flip) for i in range(size)])


def count_rounds(values):
    steps = [(1 << bit, 0) for bit in range(1, dp_bits())] + [(0, 1)]
    rounds = [[(1, 0)]] + [steps[at : at + 2] for at in range(0, len(steps), 2)]
    for group in rounds:
        flips = list(group)
        if len(group) == 2:
            flips.append((group[0][0] | group[1][0], group[0][1] | group[1][1]))
        values = values + sum(exchange(values, *flip) for flip in flips)
        yield values


def part_orders(bit_count):
    rest = list(range(3, bit_count))
    return (
        [("dp", 1), ("outer", 0), ("dp", 2)] + [("dp", b) for b in rest],
        [("outer", 0), ("dp", 2), ("dp", 1)] + [("dp", b) for b in rest],
        [("dp", 2), ("dp", 1), ("outer", 0)] + [("dp", b) for b in rest],
    )


def halve(values, dims, step):
    axis, bit = step
    place = dims.index(step)
    mine = bit_of(axis, bit)
    keep = lax.dynamic_index_in_dim(values, mine, place, keepdims=False)
    send = lax.dynamic_index_in_dim(values, 1 - mine, place, keepdims=False)
    left = dims[:place] + dims[place + 1 :]
    return keep + swap(send, axis, bit), left


def scatter_sum(matrix):
    bit_count = dp_bits()
    rows, columns = matrix.shape
    share = rows // lax.axis_size("dp")
    dims = [("dp", b) for b in range(bit_count - 1, -1, -1)] + [("outer", 0)]
    values = matrix.reshape((2,) * bit_count + (2, share // 2, columns))
    values, dims = halve(values, dims, ("dp", 0))
    third = columns // 3
    pieces = []
    for index, order in enumerate(part_orders(bit_count)):
        part = lax.slice_in_dim(values, index * third, (index + 1) * third, axis=values.ndim - 1)
        left = dims
        for step in order:
            part, left = halve(part, left, step)
        pieces.append(part)
    mine = jnp.concatenate(pieces, axis=1)
    other = swap(mine, "outer", 0)
    first = lax.axis_index("outer") == 0
    return jnp.concatenate([jnp.where(first, mine, other), jnp.where(first, other, mine)], axis=0)


def per_device(
    patches,
    lengths,
    leads,
    counts,
    cotangent,
    norm1_gain,
    norm1_bias,
    lead_table,
    w_qkv,
    bias_query,
    bias_value,
    w_out,
    bias_out,
    norm2_gain,
    norm2_bias,
    w_up,
    bias_up,
    w_down,
    bias_down,
):
    slots, rows, width = patches.shape
    total = slots * rows
    hidden = w_up.shape[1]
    lead_count = lead_table.shape[0]
    steps = hidden // width
    f32, bf16 = jnp.float32, jnp.bfloat16
    parts = lax.axis_size("dp")
    share = width // parts
    fast = parts == 16 and share % 16 == 0 and slots == 4

    smem = pl.BlockSpec(memory_space=pltpu.SMEM)
    params = pltpu.CompilerParams(vmem_limit_bytes=VMEM_BYTES)

    def whole(*shape):
        return pl.BlockSpec(shape, lambda *i: (0,) * len(shape))

    def by_window(columns, at=0):
        return pl.BlockSpec((rows, columns), lambda i: (i, at))

    current = [""]

    def call(kernel, grid, inputs, outs, scratch=(), after=(), carry=()):
        count, extra, carried = len(inputs), len(after) + len(carry), len(carry)
        made = count + extra + len(outs)

        def body(*refs):
            kernel(*refs[:count], *refs[count + extra : made], *refs[made + carried :])

        anywhere = pl.BlockSpec(memory_space=pl.ANY)
        return pl.pallas_call(
            body,
            grid=grid,
            in_specs=[spec for spec, _ in inputs] + [anywhere] * extra,
            out_specs=[spec for spec, _, _ in outs] + [anywhere] * carried,
            out_shape=[jax.ShapeDtypeStruct(shape, dtype) for _, shape, dtype in outs]
            + [jax.ShapeDtypeStruct(value.shape, value.dtype) for value in carry],
            input_output_aliases={
                count + len(after) + i: len(outs) + i for i in range(carried)
            },
            scratch_shapes=scratch,
            compiler_params=params,
            cost_estimate=pl.CostEstimate(
                flops=int(COSTS.get(current[0], 0) * 1.15e9), bytes_accessed=0, transcendentals=0
            ),
        )(*[value for _, value in inputs], *after, *carry)

    live = jnp.arange(slots, dtype=jnp.int32) < counts[0]
    onehot = (leads[:, None] == jnp.arange(lead_count, dtype=jnp.int32)[None, :]).astype(f32)
    rounds = count_rounds(jnp.sum(onehot * live[:, None].astype(f32), axis=0))
    counted = next(rounds)

    outer_at = lax.axis_index("outer")
    bits = jnp.stack([bit_of("dp", b) for b in (3, 2, 1)] + [outer_at, bit_of("dp", 0)])
    here = bits
    def flat(vector):
        return whole(*vector.shape), vector

    by_slot = pl.BlockSpec((1, rows, width), lambda i: (i, 0, 0))
    by_head = pl.BlockSpec((1, 16, rows), lambda i: (i, 0, 0))

    def halves(blocks, columns, grid_axis=None):
        if not fast:
            spec = pl.BlockSpec((width, columns), lambda i: (0, 0))
            return [(spec, (width, columns), f32), (whole(8, 128), (8, 128), f32)]
        shape = (parts // 2, share, columns)
        return [(whole(*shape), shape, f32)] * 2

    normed, qkv = call(
        project_kernel,
        (slots,),
        [
            (smem, leads),
            (by_slot, patches),
            flat(norm1_gain),
            flat(norm1_bias),
            flat(bias_query),
            flat(bias_value),
            (whole(*lead_table.shape), lead_table),
            (whole(*w_qkv.shape), w_qkv),
        ],
        [
            (by_window(width), (total, width), bf16),
            (by_window(3 * width), (total, 3 * width), bf16),
        ],
        after=[counted],
    )
    counted = next(rounds)
    attended, residual, normed2, turned, log_total = call(
        attend_kernel,
        (slots,),
        [
            (smem, lengths),
            (by_slot, patches),
            (by_window(3 * width), qkv),
            (whole(*w_out.shape), w_out),
            flat(bias_out),
            flat(norm2_gain),
            flat(norm2_bias),
        ],
        [
            (by_window(width), (total, width), bf16),
            (by_window(width), (total, width), f32),
            (by_window(width), (total, width), bf16),
            (pl.BlockSpec((width, rows), lambda i: (0, i)), (width, total), bf16),
            (by_head, (slots, 16, rows), f32),
        ],
        after=[counted],
    )
    for counted in rounds:
        pass
    window_total = jnp.sum(onehot * counted[None, :], axis=1)
    scales = jnp.where(live, 1.0 / jnp.maximum(window_total, 1.0), 0.0)

    by_lanes = pl.BlockSpec((total, width), lambda i: (0, i))
    up_spec = pl.BlockSpec((width, width), lambda i: (0, i))
    if fast:
        pair_share = hidden // parts
        pair_shape = (parts // 2, pair_share, width)
        pair_spec = pl.BlockSpec((parts // 2 // steps, pair_share, width), lambda i: (i, 0, 0))
        down_halves = [(pair_spec, pair_shape, f32)] * 2
    else:
        down_spec = pl.BlockSpec((width, width), lambda i: (i, 0))
        down_halves = [(down_spec, (hidden, width), f32), (whole(8, 128), (8, 128), f32)]
    activated, slope, grad_down, keep_down, send_down = call(
        mlp_kernel,
        (steps,),
        [
            (smem, lengths),
            (smem, scales),
            (smem, here),
            (whole(*cotangent.shape), cotangent),
            (whole(total, width), normed2),
            (up_spec, w_up),
            flat(bias_up),
        ],
        [
            (by_lanes, (total, hidden), bf16),
            (by_lanes, (total, hidden), bf16),
            (whole(total, width), (total, width), bf16),
        ]
        + down_halves,
    )
    if fast:
        shape = (parts // 2, share, hidden)
        up_halves = [(pl.BlockSpec((parts // 2, share, width), lambda i: (0, 0, i)), shape, f32)] * 2
    else:
        up_halves = [(up_spec, (width, hidden), f32), (whole(8, 128), (8, 128), f32)]
    grad_bias_up, grad_normed2, keep_up, send_up = call(
        mlp_back_kernel,
        (steps,),
        [
            (smem, here),
            (whole(total, width), grad_down),
            (by_lanes, slope),
            (whole(width, total), turned),
            (up_spec, w_up),
            (pl.BlockSpec((width, width), lambda i: (i, 0)), w_down),
        ],
        [
            (pl.BlockSpec((1, 1, width), lambda i: (i, 0, 0)), (steps, 1, width), f32),
            (whole(total, width), (total, width), f32),
        ]
        + up_halves,
    )

    def core_swap(send):
        return swap(send, "dp", 0) if fast else send

    def split_round(pairs, dims, parts, axes, done, rider=None):
        riders = "join" if rider is not None else None
        merge = len(set(axes)) == 1 and len({tuple(dims[p[0][0]]) for p in parts}) == 1
        gridded = all(d[0] == Z1 and len(d) > 1 for d in dims) and Z1 not in axes and not riders
        rows_here = pairs[0][0].shape[-2]
        widths = [sum(width for _, _, width in part) for part in parts]
        left = [[d for d in dims[part[0][0]] if d != axis] for part, axis in zip(parts, axes)]
        if merge:
            widths, left = [sum(widths)], left[:1]
            if riders == "join":
                widths = [widths[0] + 2 * rider.shape[-1]]
        shapes = [(2,) * len(d) + (rows_here, width) for d, width in zip(left, widths)]

        def spec(shape):
            if not gridded:
                return whole(*shape)
            return pl.BlockSpec((1,) + shape[1:], lambda i: (i,) + (0,) * (len(shape) - 1))

        inputs = [(smem, bits)] + [(spec(v.shape), v) for pair in pairs for v in pair]
        if riders == "join":
            inputs.append((spec(rider.shape), rider))
        outs = [(spec(shape), shape, f32) for shape in shapes for _ in range(2)]

        def kernel(*refs):
            split_kernel(dims, parts, axes, merge, gridded, riders, *refs)

        def finish(values):
            done([(values[2 * i], values[2 * i + 1]) for i in range(len(shapes))], left)
            return list(values)

        return kernel, (2,) if gridded else (), inputs, outs, [], finish

    class Chunk:
        def __init__(self, sources, orders, shares):
            self.sources, self.orders, self.step_count = sources, orders, 0
            self.columns = [[] for _ in orders]
            for i, cuts in enumerate(shares):
                start = 0
                for pieces, width in zip(self.columns, cuts):
                    pieces.append((i, start, width))
                    start += width

        def open(self):
            shaped = lambda v: v.reshape((2, 2, 2, 2, -1, v.shape[-1]))
            pairs = [(shaped(keep), shaped(come)) for keep, come in self.sources]
            axes = [order[0] for order in self.orders]
            dims = [[Z1, Z0, X, Y]] * len(pairs)
            return split_round(pairs, dims, self.columns, axes, self.put)

        def put(self, states, dims):
            self.states, self.dims = states, dims
            self.axes = [order[self.step_count] for order in self.orders][: len(states)]
            self.step_count += 1

        def pairs(self):
            return [
                (keep, swap(send, *LINKS[axis]))
                for (send, keep), axis in zip(self.states, self.axes)
            ]

        def step(self, rider=None):
            pairs = self.pairs()
            axes = [order[self.step_count] for order in self.orders][: len(pairs)]
            parts = [[(i, 0, keep.shape[-1])] for i, (keep, _) in enumerate(pairs)]
            return split_round(pairs, self.dims, parts, axes, self.put, rider)

        def add(self):
            ((keep, come),) = self.pairs()
            spec = whole(*keep.shape)

            def finish(values):
                (self.own,) = values
                return values

            inputs = [(spec, keep), (spec, come)]
            return add_kernel, (), inputs, [(spec, keep.shape, f32)], [], finish

        def place(self, outputs, finish, rider=False):
            own = self.own
            other = swap(own, *LINKS[Y])
            moves, start = [], 0
            for pieces in self.columns:
                for source, first, wide in pieces:
                    for out, (origin, low, size) in enumerate(outputs):
                        begin, end = max(first, low), min(first + wide, low + size)
                        if origin == source and begin < end:
                            moves.append((out, begin - low, start + begin - first, end - begin))
                    start += wide
            shapes = [(2 * own.shape[0], size) for _, _, size in outputs]
            if rider:
                shapes.append((2 * own.shape[0], (own.shape[1] - start) // 2))

            def kernel(*refs):
                place_kernel(moves, start if rider else None, *refs)

            inputs = [(smem, bits), (whole(*own.shape), own), (whole(*other.shape), other)]
            outs = [(whole(*shape), shape, f32) for shape in shapes]
            return kernel, (), inputs, outs, [], finish

    come_down = core_swap(send_down)
    come_up = core_swap(send_up)
    made = {}

    def keep_results(*names):
        def finish(values):
            made.update(zip(names, values))
            return list(values[:1])

        return finish

    def middle():
        return (
            middle_back_kernel,
            (slots,),
            [
                (smem, lengths),
                (smem, scales),
                (smem, here),
                (by_slot, cotangent),
                (by_window(width), residual),
                (by_window(width), grad_normed2),
                (by_window(width), attended),
                (whole(*w_out.shape), w_out),
                flat(norm2_gain),
            ],
            [
                (by_window(width), (total, width), f32),
                (by_window(width), (total, width), bf16),
                (by_head, (slots, 16, rows), f32),
                (whole(8, width), (8, width), f32),
                (by_window(width), (total, width), bf16),
            ],
            [],
            keep_results("grad_residual", "grad_attended", "delta", "sums", "branch"),
        )

    half = width // 2

    def attention_first():
        return (
            attend_back_first_kernel,
            (slots,),
            [
                (smem, lengths),
                (by_window(half, 0), qkv),
                (by_window(half, 2), qkv),
                (by_window(half, 4), qkv),
                (by_window(half, 0), made["grad_attended"]),
                (by_head, log_total),
                (by_head, made["delta"]),
            ],
            [(by_window(3 * half), (total, 3 * half), bf16)],
            [],
            keep_results("projected_first"),
        )

    def attention():
        return (
            attend_back_kernel,
            (slots,),
            [
                (smem, lengths),
                (smem, here),
                (by_window(half, 1), qkv),
                (by_window(half, 3), qkv),
                (by_window(half, 5), qkv),
                (by_window(half, 1), made["grad_attended"]),
                (by_window(width), normed),
                (by_head, log_total),
                (by_head, made["delta"]),
                (by_window(width), attended),
                (by_window(width), made["branch"]),
                (by_window(3 * half), made["projected_first"]),
            ],
            [
                (by_window(3 * width), (total, 3 * width), bf16),
                (whole(8, width), (8, width), f32),
            ]
            + halves(parts // 2, 4 * width),
            [pltpu.VMEM((width, 4 * width), f32)],
            keep_results("grad_projected", "bias_sums", "keep_last", "send_last"),
        )

    def first_norm():
        small_rows = 64 * width // SMALL_COLUMNS
        return (
            norm_back_kernel,
            (slots,),
            [
                (smem, leads),
                (by_slot, patches),
                (by_window(width), made["grad_residual"]),
                (by_window(3 * width), made["grad_projected"]),
                (whole(*w_qkv.shape), w_qkv),
                flat(norm1_gain),
                (whole(*made["sums"].shape), made["sums"]),
                (whole(*made["bias_sums"].shape), made["bias_sums"]),
                (whole(*grad_bias_up.shape), grad_bias_up),
            ],
            [
                (by_slot, patches.shape, bf16),
                (whole(small_rows, SMALL_COLUMNS), (small_rows, SMALL_COLUMNS), f32),
            ],
            [],
            keep_results("grad_patches", "small"),
        )

    def output():
        return (
            block_out_kernel,
            (slots,),
            [
                (by_window(hidden), activated),
                (whole(*w_down.shape), w_down),
                flat(bias_down),
                (by_window(width), residual),
            ],
            [(by_slot, patches.shape, bf16)],
            [],
            keep_results("block_out"),
        )

    def add_small(bit):
        small = made["small"]
        spec = whole(*small.shape)
        inputs = [(spec, small), (spec, swap(small, "dp", bit))]
        return add_kernel, (), inputs, [(spec, small.shape, f32)], [], keep_results("small")

    def small_outs():
        small = made["small"]
        spec = whole(*small.shape)
        shapes = [(width,)] * 8 + [bias_up.shape, lead_table.shape]
        outs = [(whole(*shape), shape, f32) for shape in shapes]
        inputs = [(spec, small), (spec, swap(small, "dp", 0))]
        return small_out_kernel, (), inputs, outs, [], keep_results(*SMALL_NAMES)

    def run(works, after):
        counts = [[len(work[part]) for work in works] for part in (2, 3, 4)]

        def kernel(*refs):
            at = 0
            groups = [[] for _ in works]
            for part in counts:
                for group, count in zip(groups, part):
                    group.extend(refs[at : at + count])
                    at += count
            for work, group in zip(works, groups):
                work[0](*group)

        joined = [[item for work in works for item in work[part]] for part in (2, 3, 4)]
        values = call(kernel, works[0][1], *joined, after=after)
        tokens, at = [], 0
        for work, count in zip(works, counts[1]):
            tokens += work[5](values[at : at + count])
            at += count
        return tokens

    def build(event):
        name, step = event[0], event[1:]
        if event in PLAIN:
            works = (middle, attention_first, attention, first_norm, output)
            return works[PLAIN.index(event)]()
        if name == "S":
            return small_outs() if step == "O" else add_small({"X": 1, "Z": 2}[step])
        if step == "O":
            keep, send, orders, shares = {
                "D": (keep_down, send_down, DOWN_ORDERS, DOWN_SHARES),
                "U": (keep_up, send_up, UP_ORDERS, UP_SHARES),
                "Q": (made.get("keep_last"), made.get("send_last"), LAST_ORDERS, LAST_SHARES),
            }[name]
            chunks[name] = Chunk([(keep, core_swap(send))], orders, [shares])
            return chunks[name].open()
        chunk = chunks[name]
        if step == "A":
            return chunk.add()
        if event == "DP":
            return chunk.place([(0, 0, width)], keep_results("sum_down", "small"), rider=True)
        if event == "UP":
            return chunk.place([(0, 0, hidden)], keep_results("sum_up"))
        if event == "QP":
            outputs = [(0, 0, 3 * width), (0, 3 * width, width)]
            return chunk.place(outputs, keep_results("sum_qkv", "sum_out"))
        return chunk.step(made["small"] if event == "D4" else None)

    chunks = {}
    tokens = [grad_normed2]
    for group in SEQUENCE if fast else PLAIN:
        current[0] = group
        tokens = run([build(event) for event in group.split("+")], tokens)
    if not fast:
        for bit in range(1, dp_bits()):
            made["small"] = made["small"] + swap(made["small"], "dp", bit)
        made["small"] = made["small"] + swap(made["small"], "outer", 0)
        run([small_outs()], ())
        made["sum_down"] = scatter_sum(keep_down)
        made["sum_up"] = scatter_sum(keep_up)
        joined = scatter_sum(made["keep_last"])
        made["sum_qkv"], made["sum_out"] = joined[:, : 3 * width], joined[:, 3 * width :]
    return tuple(made[name] for name in OUTPUTS)


def solution(mesh):
    split = P(("dp", "outer"))
    placed = (split,) * 5 + (P(),) * 14
    row = P("dp", None)
    outs = (split, split, P(), P(), P(), row, P(), P(), row, P(), P(), P(), row, P(), row, P())
    return jax.shard_map(
        per_device, mesh=mesh, in_specs=placed, out_specs=outs, check_vma=False
    )
```
